512 devices in a mesh: ctx: 32 (over y_hi, z), tp: 16 (over x, y_lo, core).
Axes of the slice: x: 4, y: 4 (y_hi: 2, y_lo: 2; y = y_hi * 2 + y_lo), z: 16, core: 2. Of those that a mesh axis runs over, the one named last changes fastest.
Arguments:
- queries: bfloat16 [4096, 12288], P('ctx', 'tp'), may hold values from -8 to 8
- keys: bfloat16 [4096, 1024], P('ctx'), may hold values from -16 to 16
- values: bfloat16 [4096, 1024], P('ctx'), may hold values from -6 to 6
- doc_ids: int32 [4096], replicated, may hold values from 0 to 3, never falling along the last dimension, each value on 1 to 2560 neighbouring positions
- replica_of: int32 [4], replicated, may hold values from 0 to 31, as said below
- step_query: bfloat16 [4, 12288], P(None, 'tp'), may hold values from -8 to 8
- step_key: bfloat16 [4, 1024], replicated, may hold values from -16 to 16
- step_value: bfloat16 [4, 1024], replicated, may hold values from -6 to 6
- out_weight: bfloat16 [12288, 12288], P('tp', 'ctx'), may hold values from -0.0546875 to 0.0546875
Outputs:
- context: bfloat16 [4096, 12288], P('ctx', 'tp')
- next_hidden: bfloat16 [32, 12288], P(None, 'ctx')
- replica_keys: bfloat16 [32, 1024, 2560], P('ctx', 'tp')
- replica_values: bfloat16 [32, 1024, 2560], P('ctx', 'tp')
The draws below stay inside these ranges and needn't reach their ends.
Inputs may be any that keep to these rules, and one draw needn't show every extreme that they name: `doc_ids`: documents occupy whole runs of positions in rising order; each has 1 to 2560 positions, and one has exactly 2560. `replica_of`: the documents name distinct replicas.
All inputs are finite; a program needn't handle non-finite values.
Results may differ from the reference program's by a relative error of at most 0.02.
Values may be sent and summed in bfloat16 or wider, within the bound.
No kernel may reach another device: no remote copies, remote signals or barrier semaphores. Data moves between devices by JAX's collectives and lax.ppermute only.
A program may use at most 64 MiB of HBM per device.

```python
import math
import jax
import jax.numpy as jnp
import numpy as np
from jax import lax

D = 12288
H = 96
KVH = 8
HD = 128
NDOC = 4
TOKENS = 4096
MOST = 2560
N_CTX = 32


def draw_queries(key, part):
    key = jax.random.fold_in(key, 11)
    result = jnp.clip(jax.random.normal(key, (TOKENS, D), jnp.float32), -6.0, 6.0)
    return result.astype(jnp.bfloat16)


def draw_keys(key, part):
    key = jax.random.fold_in(key, 12)
    result = jnp.clip(3.0 * jax.random.normal(key, (TOKENS, KVH * HD), jnp.float32), -15.0, 15.0)
    return result.astype(jnp.bfloat16)


def draw_step_query(key, part):
    key = jax.random.fold_in(key, 13)
    result = jnp.clip(jax.random.normal(key, (NDOC, D), jnp.float32), -6.0, 6.0)
    return result.astype(jnp.bfloat16)


def draw_replica_of(key, part):
    key = jax.random.fold_in(key, 14)
    first_key, second_key = jax.random.split(key)
    shuffled = jax.random.permutation(first_key, N_CTX).astype(jnp.int32)
    last_slot = jnp.argmax(shuffled == N_CTX - 1).astype(jnp.int32)
    shift_by = jax.random.randint(second_key, (), 0, NDOC, dtype=jnp.int32)
    return jnp.roll(shuffled, shift_by - last_slot)[:NDOC].astype(jnp.int32)


def steps_of(key, dims, cuts, smallest, largest):
    gain, own = 1.0, jax.random.fold_in(key, 6)
    for dim, blocks in cuts:
        heights = jnp.exp(jax.random.uniform(jax.random.fold_in(own, dim), (blocks,), jnp.float32, smallest / len(cuts), largest / len(cuts)))
        gain = gain * jnp.repeat(heights, dims[dim] // blocks).reshape([-1 if axis == dim else 1 for axis in range(len(dims))])
    return gain


def length_profile(number_of, total, reach, skew):
    weights = [(1 << 20) // math.isqrt(standing ** skew) + 1 for standing in range(2, number_of + 1)]
    rest, given = total - reach - (number_of - 1), [1] * (number_of - 1)
    while rest > 0:
        candidates = [i for i in range(number_of - 1) if given[i] < reach]
        pool, left = sum([weights[i] for i in candidates]), rest
        for i in candidates:
            more = min(reach - given[i], max(1, left * weights[i] // pool), rest)
            given[i] = given[i] + more
            rest = rest - more
    return np.array([reach] + given)


def ragged_sizes(key, number_of, total, limit, lean):
    if number_of == 2:
        one = jax.random.randint(key, (), max(1, total - limit), min(limit, total - 1) + 1)
        return jnp.stack([one, total - one])
    tallies = jnp.asarray(length_profile(number_of, total, limit, lean), jnp.int32)
    pairs = (number_of - 1) // 2
    giver, taker = tallies[1:1 + 2 * pairs:2], tallies[2:2 + 2 * pairs:2]
    margin = jnp.minimum(giver - 1, limit - taker)
    shifted = jax.random.randint(jax.random.fold_in(key, 1), (pairs,), 0, 1 << 20) % (margin + 1)
    tallies = tallies.at[1:1 + 2 * pairs:2].set(giver - shifted).at[2:2 + 2 * pairs:2].set(taker + shifted)
    return tallies[jax.random.permutation(jax.random.fold_in(key, 2), number_of)]


def scatter_about(rng, shape, width, reach, shards=(), kind=jnp.bfloat16):
    values = jax.random.normal(rng, shape, jnp.float32) * width
    if len(shards) > 0:
        values = steps_of(rng, shape, shards, -0.22, 0.18) * values
    return jnp.clip(values, min=-reach, max=reach).astype(kind)


def setup_inputs(seed: int = 0) -> dict:
    key_of = jax.random.split(jax.random.key(seed), 10)
    queries = draw_queries(jax.random.fold_in(key_of[9], 71), 0)
    keys = draw_keys(jax.random.fold_in(key_of[9], 71), 0)
    values = scatter_about(key_of[2], (TOKENS, KVH * HD), 1.0, 6.0, ((0, 32),))
    doc_ids = jnp.searchsorted(jnp.cumsum(ragged_sizes(key_of[3], NDOC, TOKENS, MOST, 0)), jnp.arange(TOKENS), side="right").astype(jnp.int32)
    replica_of = draw_replica_of(jax.random.fold_in(key_of[9], 71), 0)
    step_query = draw_step_query(jax.random.fold_in(key_of[9], 71), 0)
    step_key = scatter_about(key_of[6], (NDOC, KVH * HD), 4.0, 16.0)
    step_value = scatter_about(key_of[7], (NDOC, KVH * HD), 1.0, 6.0)
    out_weight = scatter_about(key_of[8], (D, D), D ** -0.5, 0.0546875, ((0, 16), (1, 32)))
    return {"queries": queries, "keys": keys, "values": values, "doc_ids": doc_ids, "replica_of": replica_of, "step_query": step_query, "step_key": step_key, "step_value": step_value, "out_weight": out_weight}


def reference(queries, keys, values, doc_ids, replica_of, step_query, step_key, step_value, out_weight):
    group_size = H // KVH
    score_scale = 1.0 / math.sqrt(HD)
    block_rows = 64
    highest = lax.Precision.HIGHEST
    keys_wide = keys.astype(jnp.float32).reshape(TOKENS, KVH, HD)
    values_wide = values.astype(jnp.float32).reshape(TOKENS, KVH, HD)
    positions = jnp.arange(TOKENS, dtype=jnp.int32)

    def one_block(start):
        query_block = lax.dynamic_slice_in_dim(queries, start, block_rows, 0).astype(jnp.float32)
        query_block = query_block.reshape(block_rows, KVH, group_size, HD)
        query_pos = start + jnp.arange(block_rows, dtype=jnp.int32)
        query_doc = lax.dynamic_slice_in_dim(doc_ids, start, block_rows, 0)
        scores = jnp.einsum('bkgd,lkd->kgbl', query_block, keys_wide, precision=highest) * score_scale
        allowed = (doc_ids[None, :] == query_doc[:, None]) & (positions[None, :] <= query_pos[:, None])
        masked = jnp.where(allowed[None, None], scores, -1e+30)
        row_top = lax.optimization_barrier(jnp.max(masked, axis=-1))
        weights = jnp.where(allowed[None, None], jnp.exp(scores - row_top[..., None]), 0.0)
        row_total = lax.optimization_barrier(jnp.sum(weights, axis=-1))
        rounded = lax.optimization_barrier(weights.astype(jnp.bfloat16)).astype(jnp.float32)
        summed = jnp.einsum('kgbl,lkd->bkgd', rounded, values_wide, precision=highest)
        summed = summed / jnp.transpose(row_total, (2, 0, 1))[..., None]
        return summed.reshape(block_rows, D).astype(jnp.bfloat16)
    block_starts = jnp.arange(0, TOKENS, block_rows, dtype=jnp.int32)
    block_outs = lax.map(one_block, block_starts)
    context = block_outs.reshape(TOKENS, D)

    def one_doc(doc_index):
        inside = doc_ids == doc_index
        query_row = step_query[doc_index].astype(jnp.float32).reshape(KVH, group_size, HD)
        own_key = step_key[doc_index].astype(jnp.float32).reshape(KVH, HD)
        own_value = step_value[doc_index].astype(jnp.float32).reshape(KVH, HD)
        cached = jnp.einsum('kgd,lkd->kgl', query_row, keys_wide, precision=highest) * score_scale
        own_score = jnp.einsum('kgd,kd->kg', query_row, own_key, precision=highest) * score_scale
        row_top = jnp.maximum(lax.optimization_barrier(jnp.max(jnp.where(inside[None, None], cached, -1e+30), axis=-1)), own_score)
        weights = jnp.where(inside[None, None], jnp.exp(cached - row_top[..., None]), 0.0)
        own_prob = jnp.exp(own_score - row_top)
        row_total = lax.optimization_barrier(jnp.sum(weights, axis=-1)) + own_prob
        rounded = lax.optimization_barrier(weights.astype(jnp.bfloat16)).astype(jnp.float32)
        own_rounded = lax.optimization_barrier(own_prob.astype(jnp.bfloat16)).astype(jnp.float32)
        summed = jnp.einsum('kgl,lkd->kgd', rounded, values_wide, precision=highest)
        summed = summed + own_rounded[..., None] * own_value[:, None, :]
        return (summed / row_total[..., None]).reshape(D).astype(jnp.bfloat16)
    attended = lax.map(one_doc, jnp.arange(NDOC, dtype=jnp.int32))
    replica_hot = (replica_of[None, :] == jnp.arange(N_CTX, dtype=jnp.int32)[:, None]).astype(jnp.float32)
    placed = jnp.dot(replica_hot, attended.astype(jnp.float32), precision=highest).astype(jnp.bfloat16)
    next_hidden = jnp.dot(placed, out_weight, preferred_element_type=jnp.float32).astype(jnp.bfloat16)
    doc_numbers = jnp.arange(NDOC, dtype=jnp.int32)

    def one_replica(replica):
        match_rows = (replica_of == replica).astype(jnp.int32)
        has_request = jnp.sum(match_rows) > 0
        chosen_doc = jnp.sum(match_rows * doc_numbers)
        doc_start = jnp.sum((doc_ids < chosen_doc).astype(jnp.int32))
        doc_length = jnp.sum((doc_ids == chosen_doc).astype(jnp.int32))
        slots = jnp.arange(MOST, dtype=jnp.int32)
        live = (slots < doc_length) & has_request
        source_rows = jnp.clip(doc_start + slots, 0, TOKENS - 1).astype(jnp.int32)
        slot_keys = jnp.where(live[:, None], jnp.take(keys, source_rows, axis=0), jnp.zeros((), keys.dtype))
        slot_values = jnp.where(live[:, None], jnp.take(values, source_rows, axis=0), jnp.zeros((), values.dtype))
        return (jnp.transpose(slot_keys, (1, 0)), jnp.transpose(slot_values, (1, 0)))
    replica_keys, replica_values = lax.map(one_replica, jnp.arange(N_CTX, dtype=jnp.int32))
    return (context, next_hidden, replica_keys, replica_values)
```

```python
import math

import jax
import jax.numpy as jnp
import numpy as np
from jax import lax
from jax.experimental import pallas as pl
from jax.experimental.pallas import tpu as pltpu
from jax.sharding import Mesh
from jax.sharding import PartitionSpec as P

H = 96
KVH = 8
HD = 128
NDOC = 4
ROWS = 128
NB = 32
MOST = 2560
HEADS = 6
SCALE = 1.0 / math.sqrt(HD)
CTX = ("yh", "z1", "z0")
TP = ("x", "yl", "c")
NEG = -1e30


def pick_kernel(meta, keys, values, out):
    out[...] = jnp.where(meta[1] == 0, keys[...], values[...])


def pick(meta, keys, values):
    head = pl.BlockSpec((ROWS, HD), lambda i, m: (0, m[2]))
    return pl.pallas_call(
        pick_kernel,
        out_shape=jax.ShapeDtypeStruct((ROWS, HD), jnp.bfloat16),
        grid_spec=pltpu.PrefetchScalarGridSpec(
            num_scalar_prefetch=1,
            grid=(1,),
            in_specs=[head, head],
            out_specs=pl.BlockSpec((ROWS, HD), lambda i, m: (0, 0)),
        ),
        name="pick",
    )(meta, keys, values)


def attend_kernel(
    meta, replica_of, doc_ids, queries, step_query, step_key, step_value, weight,
    own0, own1, own2, own3, own4, got0, got1, got2, got3, got4,
    context, terms, replica_keys, replica_values,
    cache, q48, top, total, acc,
):
    ctx, core, z0 = meta[0], meta[1], meta[3]
    classes = ((own0, got0, 0, 0, 8), (own1, got1, 3, 0, 8), (own2, got2, 1, 0, 8), (own3, got3, 2, 0, 4), (own4, got4, 2, 4, 8))
    for own, got, shift, first, last in classes:
        rest = lax.rem(z0 + shift, 4)
        for g in range(first, last):
            cache[core, (g // 4) * 16 + (g % 4) * 4 + rest] = own[g - first]
            cache[1 - core, (g // 4) * 16 + (g % 4) * 4 + rest] = got[g - first]
    cache[:, NB] = jnp.zeros((2, ROWS, HD), jnp.bfloat16)
    ids = doc_ids[...]
    starts = [jnp.int32(0)] + [jnp.sum((ids < d).astype(jnp.int32)) for d in range(1, NDOC)]
    ends = starts[1:] + [jnp.int32(NB * ROWS)]

    q48[...] = jnp.zeros_like(q48)
    steps = step_query[...].astype(jnp.float32)
    for h in range(HEADS):
        q48[h * 8 : h * 8 + NDOC, :] = steps[:, h * HD : (h + 1) * HD]
    q = q48[...]
    pad = jnp.zeros((8 - NDOC, HD), jnp.float32)
    own_key = jnp.concatenate([step_key[...].astype(jnp.float32), pad] * HEADS, axis=0)
    own_value = jnp.concatenate([step_value[...].astype(jnp.float32), pad] * HEADS, axis=0)
    doc_row = lax.broadcasted_iota(jnp.int32, (HEADS * 8, 1), 0) % 8
    low = jnp.full((HEADS * 8, 1), NB * ROWS, jnp.int32)
    high = jnp.zeros((HEADS * 8, 1), jnp.int32)
    for d in range(NDOC):
        low = jnp.where(doc_row == d, starts[d], low)
        high = jnp.where(doc_row == d, ends[d], high)
    all_keys = cache[0, :NB].reshape(NB * ROWS, HD)
    all_values = cache[1, :NB].reshape(NB * ROWS, HD)
    nums = lax.dot_general(q.astype(jnp.bfloat16), all_keys, (((1,), (1,)), ((), ())), preferred_element_type=jnp.float32)
    nums = nums * SCALE
    place = lax.broadcasted_iota(jnp.int32, (HEADS * 8, NB * ROWS), 1)
    nums = jnp.where((place >= low) & (place < high), nums, NEG)
    own_score = jnp.sum(q * own_key, axis=1, keepdims=True) * SCALE
    step_top = jnp.maximum(jnp.max(nums, axis=1, keepdims=True), own_score)
    probs = jnp.exp(nums - step_top)
    own_prob = jnp.exp(own_score - step_top)
    step_total = jnp.sum(probs, axis=1, keepdims=True) + own_prob
    mixed = jnp.dot(probs.astype(jnp.bfloat16), all_values, preferred_element_type=jnp.float32)
    mixed = mixed + own_prob.astype(jnp.bfloat16).astype(jnp.float32) * own_value
    attended = mixed / step_total
    wide = jnp.concatenate([attended[h * 8 : (h + 1) * 8, :] for h in range(HEADS)], axis=1)
    term = jnp.dot(wide.astype(jnp.bfloat16), weight[...], preferred_element_type=jnp.float32)
    for k in range(16):
        terms[k] = term

    row = ctx * ROWS + lax.broadcasted_iota(jnp.int32, (ROWS, 1), 0)
    row_start = jnp.zeros((ROWS, 1), jnp.int32)
    first = jnp.int32(0)
    for d in range(1, NDOC):
        row_start = jnp.where(row >= starts[d], starts[d], row_start)
        first = jnp.where(ctx * ROWS >= starts[d], starts[d], first)
    top[...] = jnp.full_like(top, NEG)
    total[...] = jnp.zeros_like(total)
    acc[...] = jnp.zeros_like(acc)
    block0 = first // ROWS
    factor = SCALE * math.log2(math.e)

    def chunk(i, carry):
        at = block0 + 2 * i
        key2 = cache[0, pl.ds(at, 2)].reshape(2 * ROWS, HD)
        value2 = cache[1, pl.ds(at, 2)].reshape(2 * ROWS, HD)
        col = at * ROWS + lax.broadcasted_iota(jnp.int32, (ROWS, 2 * ROWS), 1)
        allowed = (col <= row) & (col >= row_start)
        for h in range(HEADS):
            part = queries[:, h * HD : (h + 1) * HD]
            s = lax.dot_general(part, key2, (((1,), (1,)), ((), ())), preferred_element_type=jnp.float32)
            s = jnp.where(allowed, s * factor, NEG)
            old = top[h]
            new = jnp.maximum(old, jnp.max(s, axis=1, keepdims=True))
            p = jnp.exp2(s - new[:, :1])
            alpha = jnp.exp2(old - new)
            total[h] = total[h] * alpha + jnp.sum(p, axis=1, keepdims=True)
            acc[h] = acc[h] * alpha + jnp.dot(p.astype(jnp.bfloat16), value2, preferred_element_type=jnp.float32)
            top[h] = new
        return carry

    lax.fori_loop(0, (ctx - block0 + 2) // 2, chunk, 0)
    for h in range(HEADS):
        context[:, h * HD : (h + 1) * HD] = (acc[h] / total[h]).astype(jnp.bfloat16)

    asked = jnp.int32(0)
    start = jnp.int32(0)
    length = jnp.int32(0)
    for d in range(NDOC):
        mine = replica_of[d] == ctx
        asked = jnp.where(mine, 1, asked)
        start = jnp.where(mine, starts[d], start)
        length = jnp.where(mine, ends[d] - starts[d], length)

    @pl.when(asked == 0)
    def _():
        replica_keys[...] = jnp.zeros_like(replica_keys)
        replica_values[...] = jnp.zeros_like(replica_values)

    @pl.when(asked == 1)
    def _():
        offset = lax.rem(start, ROWS)
        begin = start // ROWS
        r = lax.broadcasted_iota(jnp.int32, (2 * ROWS, ROWS), 0)
        s = lax.broadcasted_iota(jnp.int32, (2 * ROWS, ROWS), 1)
        hot = (r == s + offset).astype(jnp.bfloat16)
        slot = lax.broadcasted_iota(jnp.int32, (HD // 2, ROWS), 1)
        for i in range(MOST // ROWS):
            at = jnp.minimum(begin + i, NB - 1)
            live = slot + i * ROWS < length
            for which, out in ((0, replica_keys), (1, replica_values)):
                source = cache[which, pl.ds(at, 2)].reshape(2 * ROWS, HD)
                moved = lax.dot_general(source, hot, (((0,), (0,)), ((), ())), preferred_element_type=jnp.float32)
                moved = jnp.where(core == 0, moved[: HD // 2], moved[HD // 2 :])
                out[:, i * ROWS : (i + 1) * ROWS] = jnp.where(live, moved, 0.0).astype(jnp.bfloat16)


def attend(meta, replica_of, doc_ids, queries, step_query, step_key, step_value, weight, own, got):
    def whole(x):
        return pl.BlockSpec(x.shape, lambda i, m, n, nd=len(x.shape): (0,) * nd)

    head = pl.BlockSpec((NDOC, HD), lambda i, m, n: (0, m[2]))
    outs = (
        jax.ShapeDtypeStruct((ROWS, HEADS * HD), jnp.bfloat16),
        jax.ShapeDtypeStruct((16, 8, weight.shape[1]), jnp.float32),
        jax.ShapeDtypeStruct((HD // 2, MOST), jnp.bfloat16),
        jax.ShapeDtypeStruct((HD // 2, MOST), jnp.bfloat16),
    )
    return pl.pallas_call(
        attend_kernel,
        out_shape=outs,
        grid_spec=pltpu.PrefetchScalarGridSpec(
            num_scalar_prefetch=2,
            grid=(1,),
            in_specs=[whole(doc_ids), whole(queries), whole(step_query), head, head, whole(weight)] + [whole(x) for x in own + got],
            out_specs=[whole(x) for x in outs],
            scratch_shapes=[
                pltpu.VMEM((2, NB + 1, ROWS, HD), jnp.bfloat16),
                pltpu.VMEM((HEADS * 8, HD), jnp.float32),
                pltpu.VMEM((HEADS, ROWS, HD), jnp.float32),
                pltpu.VMEM((HEADS, ROWS, HD), jnp.float32),
                pltpu.VMEM((HEADS, ROWS, HD), jnp.float32),
            ],
        ),
        compiler_params=pltpu.CompilerParams(vmem_limit_bytes=40 * 1024 * 1024),
        name="attend",
    )(meta, replica_of, doc_ids, queries, step_query, step_key, step_value, weight, *own, *got)


def local(queries, keys, values, doc_ids, replica_of, step_query, step_key, step_value, out_weight):
    x, yl, core = lax.axis_index("x"), lax.axis_index("yl"), lax.axis_index("c")
    z0 = lax.axis_index("z0")
    ctx = lax.axis_index("yh") * 16 + lax.axis_index("z1") * 4 + z0
    meta = jnp.stack([ctx, core, x * 2 + yl, z0]).astype(jnp.int32)
    mine = pick(meta, keys, values)

    def along_z(a, by):
        return lax.ppermute(a, ("z1", "z0"), [(i, (i + by) % 16) for i in range(16)])

    def across(a):
        return lax.ppermute(a, "c", [(0, 1), (1, 0)])

    far = lax.all_to_all(jnp.broadcast_to(mine[None], (8, ROWS, HD)), ("yh", "z1"), 0, 0)
    own = [far, along_z(far, 1), along_z(far, -1), along_z(far[:4], 2), along_z(far[4:], -2)]
    got = [across(a) for a in own]
    context, terms, replica_keys, replica_values = attend(
        meta, replica_of, doc_ids.reshape(NB, ROWS), queries, step_query, step_key, step_value, out_weight, own, got
    )
    parts = lax.all_to_all(terms, TP, 0, 0)
    projected = jnp.sum(parts, axis=0)
    replicas = jnp.arange(NB, dtype=jnp.int32)
    next_hidden = jnp.zeros((NB, out_weight.shape[1]), jnp.float32)
    for d in range(NDOC):
        next_hidden = jnp.where((replicas == replica_of[d])[:, None], projected[d][None, :], next_hidden)
    return (context, next_hidden.astype(jnp.bfloat16), replica_keys[None], replica_values[None])


def solution(mesh):
    fine = Mesh(np.asarray(mesh.devices).reshape(2, 4, 4, 4, 2, 2), CTX + TP)
    placed = (
        P(CTX, TP),
        P(CTX, None),
        P(CTX, None),
        P(),
        P(),
        P(None, TP),
        P(),
        P(),
        P(TP, CTX),
    )
    return jax.shard_map(
        local,
        mesh=fine,
        in_specs=placed,
        out_specs=(P(CTX, TP), P(None, CTX), P(CTX, TP, None), P(CTX, TP, None)),
        check_vma=False,
    )
```

```python
import math

import jax
import jax.numpy as jnp
import numpy as np
from jax import lax
from jax.experimental import pallas as pl
from jax.experimental.pallas import tpu as pltpu
from jax.sharding import Mesh
from jax.sharding import PartitionSpec as P

H = 96
KVH = 8
HD = 128
NDOC = 4
ROWS = 128
NB = 32
MOST = 2560
HEADS = 6
SCALE = 1.0 / math.sqrt(HD)
CTX = ("yh", "z1", "z0")
TP = ("x", "yl", "c")
NEG = -1e30


def position():
    z0 = lax.axis_index("z0")
    ctx = lax.axis_index("yh") * 16 + lax.axis_index("z1") * 4 + z0
    return ctx, lax.axis_index("c"), lax.axis_index("x") * 2 + lax.axis_index("yl"), z0


def pick_kernel(keys, values, out, half, sem):
    _, core, head, _ = position()
    columns = pl.ds(pl.multiple_of(head * HD, HD), HD)
    for which, source in ((0, keys), (1, values)):

        @pl.when(core == which)
        def _():
            copy = pltpu.make_async_copy(source.at[:, columns], half, sem)
            copy.start()
            copy.wait()

    for g in range(8):
        out[g] = half[...]


def pick(keys, values):
    return pl.pallas_call(
        pick_kernel,
        out_shape=jax.ShapeDtypeStruct((8, ROWS, HD), jnp.bfloat16),
        in_specs=[pl.BlockSpec(memory_space=pltpu.HBM)] * 2,
        out_specs=pl.BlockSpec(memory_space=pltpu.VMEM),
        scratch_shapes=[pltpu.VMEM((ROWS, HD), jnp.bfloat16), pltpu.SemaphoreType.DMA],
        compiler_params=pltpu.CompilerParams(vmem_limit_bytes=60 * 1024 * 1024),
        name="pick",
    )(keys, values)


def doc_bounds(doc_ids):
    ids = doc_ids[...]
    starts = [jnp.int32(0)] + [jnp.sum((ids < d).astype(jnp.int32)) for d in range(1, NDOC)]
    return starts, starts[1:] + [jnp.int32(NB * ROWS)]


def decode_kernel(doc_ids, step_query, step_key, step_value, weight, far, near, across, other, terms, q48):
    _, core, head, z0 = position()
    columns = pl.ds(pl.multiple_of(head * HD, HD), HD)
    side = 1 - 2 * core
    starts, ends = doc_bounds(doc_ids)
    q48[...] = jnp.zeros_like(q48)
    steps = step_query[...].astype(jnp.float32)
    for h in range(HEADS):
        q48[h * 8 : h * 8 + NDOC, :] = steps[:, h * HD : (h + 1) * HD]
    q = q48[...]
    pad = jnp.zeros((8 - NDOC, HD), jnp.float32)
    own_key = jnp.concatenate([step_key[:, columns].astype(jnp.float32), pad] * HEADS, axis=0)
    own_value = jnp.concatenate([step_value[:, columns].astype(jnp.float32), pad] * HEADS, axis=0)
    doc_row = lax.broadcasted_iota(jnp.int32, (HEADS * 8, 1), 0) % 8
    low = jnp.full((HEADS * 8, 1), NB * ROWS, jnp.int32)
    high = jnp.zeros((HEADS * 8, 1), jnp.int32)
    for d in range(NDOC):
        low = jnp.where(doc_row == d, starts[d], low)
        high = jnp.where(doc_row == d, ends[d], high)
    narrow = q.astype(jnp.bfloat16)
    groups = (
        (far[0], far[1], 8, z0, 0),
        (near[0], near[1], 8, z0 + 4 + side, 0),
        (other[0, :8], other[1, :8], 8, z0 + 4 - side, 0),
        (across[0], across[1], 4, z0 + 2, core),
        (other[0, 8:], other[1, 8:], 4, z0 + 2, 1 - core),
    )
    nums, tops = [], []
    for keys, _, count, kind, first in groups:
        at = lax.broadcasted_iota(jnp.int32, (1, count * ROWS), 1)
        place = (at // (4 * ROWS) + first) * (16 * ROWS) + (at // ROWS % 4) * (4 * ROWS) + lax.rem(kind, 4) * ROWS + at % ROWS
        s = lax.dot_general(narrow, keys.reshape(count * ROWS, HD), (((1,), (1,)), ((), ())), preferred_element_type=jnp.float32)
        s = jnp.where((place >= low) & (place < high), s * SCALE, NEG)
        nums.append(s)
        tops.append(jnp.max(s, axis=1, keepdims=True))
    own_score = jnp.sum(q * own_key, axis=1, keepdims=True) * SCALE
    top = own_score
    for t in tops:
        top = jnp.maximum(top, t)
    own_prob = jnp.exp(own_score - top)
    total = own_prob
    mixed = own_prob.astype(jnp.bfloat16).astype(jnp.float32) * own_value
    for s, (_, values, count, _, _) in zip(nums, groups):
        p = jnp.exp(s - top)
        total = total + jnp.sum(p, axis=1, keepdims=True)
        mixed = mixed + jnp.dot(p.astype(jnp.bfloat16), values.reshape(count * ROWS, HD), preferred_element_type=jnp.float32)
    attended = mixed / total
    wide = jnp.concatenate([attended[h * 8 : (h + 1) * 8, :] for h in range(HEADS)], axis=1)
    term = jnp.dot(wide.astype(jnp.bfloat16), weight[...], preferred_element_type=jnp.float32)
    for k in range(16):
        terms[k] = term


def decode(doc_ids, step_query, step_key, step_value, weight, parts):
    return pl.pallas_call(
        decode_kernel,
        out_shape=jax.ShapeDtypeStruct((16, 8, weight.shape[1]), jnp.float32),
        scratch_shapes=[pltpu.VMEM((HEADS * 8, HD), jnp.float32)],
        compiler_params=pltpu.CompilerParams(vmem_limit_bytes=12 * 1024 * 1024),
        cost_estimate=pl.CostEstimate(flops=10**8, bytes_accessed=4 * 10**6, transcendentals=2 * 10**5),
        name="decode",
    )(doc_ids, step_query, step_key, step_value, weight, *parts)


STEP = 4


def prefill_kernel(
    replica_of, doc_ids, queries, far, near, across, other,
    context, replica_keys, replica_values,
    cache, flat, acc,
):
    ctx, core, _, z0 = position()
    side = 1 - 2 * core
    for which in range(2):
        for g in range(8):
            at = (g // 4) * 16 + (g % 4) * 4
            cache[which, at + z0] = far[which, g]
            cache[which, at + lax.rem(z0 + 4 + side, 4)] = near[which, g]
            cache[which, at + lax.rem(z0 + 4 - side, 4)] = other[which, g]
        for g in range(4):
            at = g * 4 + lax.rem(z0 + 2, 4)
            cache[which, at + core * 16] = across[which, g]
            cache[which, at + (1 - core) * 16] = other[which, 8 + g]
        for b in range(NB, NB + STEP - 1):
            cache[which, b] = jnp.zeros((ROWS, HD), jnp.bfloat16)
    starts, ends = doc_bounds(doc_ids)
    for h in range(HEADS):
        flat[h * ROWS : (h + 1) * ROWS, :] = queries[:, h * HD : (h + 1) * HD]

    row = ctx * ROWS + lax.broadcasted_iota(jnp.int32, (1, ROWS), 1)
    row_start = jnp.zeros((1, ROWS), jnp.int32)
    first = jnp.int32(0)
    for d in range(1, NDOC):
        row_start = jnp.where(row >= starts[d], starts[d], row_start)
        first = jnp.where(ctx * ROWS >= starts[d], starts[d], first)
    block0 = first // ROWS
    factor = SCALE * math.log2(math.e)
    acc[...] = jnp.zeros_like(acc)

    def step(i, carry):
        old, total = carry
        at = block0 + STEP * i
        key = cache[0, pl.ds(at, STEP)].reshape(STEP * ROWS, HD)
        value = cache[1, pl.ds(at, STEP)].reshape(STEP * ROWS, HD)
        place = at * ROWS + lax.broadcasted_iota(jnp.int32, (STEP * ROWS, ROWS), 0)
        bias = jnp.where((place <= row) & (place >= row_start), 0.0, NEG)
        s = lax.dot_general(key, flat[...], (((1,), (1,)), ((), ())), preferred_element_type=jnp.float32)
        s = s * factor + jnp.concatenate([bias] * HEADS, axis=1)
        new = jnp.maximum(old, jnp.max(s, axis=0, keepdims=True))
        p = jnp.exp2(s - new)
        alpha = jnp.exp2(old - new)
        total = total * alpha + jnp.sum(p, axis=0, keepdims=True)
        acc[...] = acc[...] * alpha + lax.dot_general(
            value, p.astype(jnp.bfloat16), (((0,), (0,)), ((), ())), preferred_element_type=jnp.float32
        )
        return new, total

    wide = (1, HEADS * ROWS)
    _, total = lax.fori_loop(
        0, (ctx - block0 + STEP) // STEP, step, (jnp.full(wide, NEG, jnp.float32), jnp.zeros(wide, jnp.float32))
    )
    mixed = acc[...] / total
    for h in range(HEADS):
        context[:, h * HD : (h + 1) * HD] = jnp.transpose(mixed[:, h * ROWS : (h + 1) * ROWS]).astype(jnp.bfloat16)

    asked = jnp.int32(0)
    start = jnp.int32(0)
    length = jnp.int32(0)
    for d in range(NDOC):
        mine = replica_of[d] == ctx
        asked = jnp.where(mine, 1, asked)
        start = jnp.where(mine, starts[d], start)
        length = jnp.where(mine, ends[d] - starts[d], length)

    @pl.when(asked == 0)
    def _():
        replica_keys[...] = jnp.zeros_like(replica_keys)
        replica_values[...] = jnp.zeros_like(replica_values)

    @pl.when(asked == 1)
    def _():
        offset = lax.rem(start, ROWS)
        begin = start // ROWS
        r = lax.broadcasted_iota(jnp.int32, (2 * ROWS, ROWS), 0)
        s = lax.broadcasted_iota(jnp.int32, (2 * ROWS, ROWS), 1)
        hot = (r == s + offset).astype(jnp.bfloat16)
        slot = lax.broadcasted_iota(jnp.int32, (HD // 2, ROWS), 1)
        for i in range(MOST // ROWS):
            at = jnp.minimum(begin + i, NB - 1)
            live = slot + i * ROWS < length
            for which, out in ((0, replica_keys), (1, replica_values)):
                source = cache[which, pl.ds(at, 2)].reshape(2 * ROWS, HD)
                moved = lax.dot_general(source, hot, (((0,), (0,)), ((), ())), preferred_element_type=jnp.float32)
                moved = jnp.where(core == 0, moved[: HD // 2], moved[HD // 2 :])
                out[:, i * ROWS : (i + 1) * ROWS] = jnp.where(live, moved, 0.0).astype(jnp.bfloat16)


def prefill(replica_of, doc_ids, queries, parts):
    vmem = pl.BlockSpec(memory_space=pltpu.VMEM)
    return pl.pallas_call(
        prefill_kernel,
        out_shape=(
            jax.ShapeDtypeStruct((ROWS, HEADS * HD), jnp.bfloat16),
            jax.ShapeDtypeStruct((HD // 2, MOST), jnp.bfloat16),
            jax.ShapeDtypeStruct((HD // 2, MOST), jnp.bfloat16),
        ),
        in_specs=[pl.BlockSpec(memory_space=pltpu.SMEM)] + [vmem] * 6,
        scratch_shapes=[
            pltpu.VMEM((2, NB + STEP - 1, ROWS, HD), jnp.bfloat16),
            pltpu.VMEM((HEADS * ROWS, HD), jnp.bfloat16),
            pltpu.VMEM((HD, HEADS * ROWS), jnp.float32),
        ],
        compiler_params=pltpu.CompilerParams(vmem_limit_bytes=16 * 1024 * 1024),
        cost_estimate=pl.CostEstimate(flops=2 * 10**9, bytes_accessed=4 * 10**6, transcendentals=2 * 10**6),
        name="prefill",
    )(replica_of, doc_ids, queries, *parts)


def finish_kernel(replica_of, summed, out):
    projected = jnp.sum(summed[...], axis=0)
    replica = lax.broadcasted_iota(jnp.int32, out.shape, 0)
    rows = jnp.zeros(out.shape, jnp.float32)
    for d in range(NDOC):
        rows = jnp.where(replica == replica_of[d], projected[d : d + 1], rows)
    out[...] = rows.astype(jnp.bfloat16)


def finish(replica_of, summed):
    return pl.pallas_call(
        finish_kernel,
        out_shape=jax.ShapeDtypeStruct((NB, summed.shape[2]), jnp.bfloat16),
        in_specs=[pl.BlockSpec(memory_space=pltpu.SMEM), pl.BlockSpec(memory_space=pltpu.VMEM)],
        compiler_params=pltpu.CompilerParams(vmem_limit_bytes=2 * 1024 * 1024),
        name="finish",
    )(replica_of, summed)


def from_sides(a, by):
    pairs = []
    for yh in range(2):
        for z in range(16):
            for t in range(16):
                core = t % 2
                source = (z + (by if core == 0 else -by)) % 16
                pairs.append(((yh * 16 + source) * 16 + t, (yh * 16 + z) * 16 + t))
    return lax.ppermute(a, CTX + TP, pairs)


def local(queries, keys, values, doc_ids, replica_of, step_query, step_key, step_value, out_weight):
    half = lax.all_to_all(pick(keys, values), ("yh", "z1"), 0, 0)
    far = lax.all_gather(half, "c", axis=0)
    near = from_sides(far, 1)
    across = from_sides(lax.dynamic_slice_in_dim(far, lax.axis_index("c") * 4, 4, 1), 2)
    both = jnp.concatenate(lax.optimization_barrier((near, across)), axis=1)
    other = lax.ppermute(both, "c", [(0, 1), (1, 0)])
    parts = [far, near, across, other]
    blocks = doc_ids.reshape(NB, ROWS)
    terms = decode(blocks, step_query, step_key, step_value, out_weight, parts)
    summed = lax.all_to_all(terms, TP, 0, 0)
    context, replica_keys, replica_values = prefill(replica_of, blocks, queries, parts)
    next_hidden = finish(replica_of, summed)
    return (context, next_hidden, replica_keys[None], replica_values[None])


def solution(mesh):
    fine = Mesh(np.asarray(mesh.devices).reshape(2, 4, 4, 4, 2, 2), CTX + TP)
    placed = (
        P(CTX, TP),
        P(CTX, None),
        P(CTX, None),
        P(),
        P(),
        P(None, TP),
        P(),
        P(),
        P(TP, CTX),
    )
    return jax.shard_map(
        local,
        mesh=fine,
        in_specs=placed,
        out_specs=(P(CTX, TP), P(None, CTX), P(CTX, TP, None), P(CTX, TP, None)),
        check_vma=False,
    )
```

```python
import math

import jax
import jax.numpy as jnp
import numpy as np
from jax import lax
from jax.experimental import pallas as pl
from jax.experimental.pallas import tpu as pltpu
from jax.sharding import Mesh
from jax.sharding import PartitionSpec as P

H = 96
KVH = 8
HD = 128
NDOC = 4
ROWS = 128
NB = 32
MOST = 2560
HEADS = 6
SCALE = 1.0 / math.sqrt(HD)
CTX = ("yh", "z1", "z0")
TP = ("x", "yl", "c")
NEG = -1e30


def position():
    z0 = lax.axis_index("z0")
    ctx = lax.axis_index("yh") * 16 + lax.axis_index("z1") * 4 + z0
    return ctx, lax.axis_index("c"), lax.axis_index("x") * 2 + lax.axis_index("yl"), z0


def pick_kernel(keys, values, out, half, sem):
    _, core, head, _ = position()
    columns = pl.ds(pl.multiple_of(head * HD, HD), HD)
    for which, source in ((0, keys), (1, values)):

        @pl.when(core == which)
        def _():
            copy = pltpu.make_async_copy(source.at[:, columns], half, sem)
            copy.start()
            copy.wait()

    for g in range(out.shape[0]):
        out[g] = half[...]


def pick(keys, values, copies):
    return pl.pallas_call(
        pick_kernel,
        out_shape=jax.ShapeDtypeStruct((copies, ROWS, HD), jnp.bfloat16),
        in_specs=[pl.BlockSpec(memory_space=pltpu.HBM)] * 2,
        out_specs=pl.BlockSpec(memory_space=pltpu.VMEM),
        scratch_shapes=[pltpu.VMEM((ROWS, HD), jnp.bfloat16), pltpu.SemaphoreType.DMA],
        compiler_params=pltpu.CompilerParams(vmem_limit_bytes=60 * 1024 * 1024),
        name="pick",
    )(keys, values)


def doc_bounds(doc_ids):
    ids = doc_ids[...]
    starts = [jnp.int32(0)] + [jnp.sum((ids < d).astype(jnp.int32)) for d in range(1, NDOC)]
    return starts, starts[1:] + [jnp.int32(NB * ROWS)]


ROW = HEADS * NDOC
PAD = 32


def decode_kernel(
    doc_ids, step_query, step_key, step_value, weight, far, near, across, other, terms, query, own_key, own_value
):
    _, core, head, z0 = position()
    columns = pl.ds(pl.multiple_of(head * HD, HD), HD)
    side = 1 - 2 * core
    starts, ends = doc_bounds(doc_ids)
    steps = step_query[...].astype(jnp.float32)
    step_keys = step_key[:, columns].astype(jnp.float32)
    step_values = step_value[:, columns].astype(jnp.float32)
    for ref in (query, own_key, own_value):
        ref[ROW:PAD, :] = jnp.zeros((PAD - ROW, HD), jnp.float32)
    for h in range(HEADS):
        rows = slice(h * NDOC, (h + 1) * NDOC)
        query[rows, :] = steps[:, h * HD : (h + 1) * HD]
        own_key[rows, :] = step_keys
        own_value[rows, :] = step_values
    q = query[...]
    document = lax.broadcasted_iota(jnp.int32, (PAD, 1), 0) % NDOC
    low = jnp.zeros((PAD, 1), jnp.int32)
    high = jnp.zeros((PAD, 1), jnp.int32)
    for d in range(NDOC):
        low = jnp.where(document == d, starts[d], low)
        high = jnp.where(document == d, ends[d], high)
    narrow = q.astype(jnp.bfloat16)
    groups = [(far, 0, z0, 0), (far, 1, z0, 1), (near, 0, z0 + 4 + side, 0), (near, 1, z0 + 4 + side, 1)]
    groups += [(other, 0, z0 + 4 - side, 0), (other, 1, z0 + 4 - side, 1), (across, 0, z0 + 2, core), (other, 2, z0 + 2, 1 - core)]
    at = lax.broadcasted_iota(jnp.int32, (1, 4 * ROWS), 1)
    at = at // ROWS * (4 * ROWS) + at % ROWS
    nums, tops = [], []
    for ref, index, kind, yh in groups:
        place = at + (yh * (16 * ROWS) + lax.rem(kind, 4) * ROWS)
        keys = ref[index, 0].reshape(4 * ROWS, HD)
        s = lax.dot_general(narrow, keys, (((1,), (1,)), ((), ())), preferred_element_type=jnp.float32)
        s = jnp.where((place >= low) & (place < high), s * SCALE, NEG)
        nums.append(s)
        tops.append(jnp.max(s, axis=1, keepdims=True))
    own_score = jnp.sum(q * own_key[...], axis=1, keepdims=True) * SCALE
    top = own_score
    for t in tops:
        top = jnp.maximum(top, t)
    own_prob = jnp.exp(own_score - top)
    total = own_prob
    mixed = own_prob.astype(jnp.bfloat16).astype(jnp.float32) * own_value[...]
    for s, (ref, index, _, _) in zip(nums, groups):
        p = jnp.exp(s - top)
        total = total + jnp.sum(p, axis=1, keepdims=True)
        values = ref[index, 1].reshape(4 * ROWS, HD)
        mixed = mixed + jnp.dot(p.astype(jnp.bfloat16), values, preferred_element_type=jnp.float32)
    query[...] = mixed / total
    wide = jnp.concatenate([query[h * NDOC : (h + 1) * NDOC, :] for h in range(HEADS)], axis=1)
    wide = jnp.concatenate([wide, jnp.zeros_like(wide)], axis=0)
    term = jnp.dot(wide.astype(jnp.bfloat16), weight[...], preferred_element_type=jnp.float32).astype(terms.dtype)
    for k in range(16):
        terms[k] = term


def decode(doc_ids, step_query, step_key, step_value, weight, parts):
    return pl.pallas_call(
        decode_kernel,
        out_shape=jax.ShapeDtypeStruct((16, 8, weight.shape[1]), jnp.bfloat16),
        scratch_shapes=[pltpu.VMEM((PAD, HD), jnp.float32)] * 3,
        compiler_params=pltpu.CompilerParams(vmem_limit_bytes=12 * 1024 * 1024),
        cost_estimate=pl.CostEstimate(flops=10**8, bytes_accessed=4 * 10**6, transcendentals=2 * 10**5),
        name="decode",
    )(doc_ids, step_query, step_key, step_value, weight, *parts)


STEP = 4


def prefill_kernel(
    replica_of, doc_ids, queries, far, near, across, other,
    context, replica_keys, replica_values,
    cache, flat, acc,
):
    ctx, core, _, z0 = position()
    side = 1 - 2 * core
    for which in range(2):
        for g in range(4):
            for yh in range(2):
                at = yh * 16 + g * 4
                cache[which, at + z0] = far[yh, which, g]
                cache[which, at + lax.rem(z0 + 4 + side, 4)] = near[yh, which, g]
                cache[which, at + lax.rem(z0 + 4 - side, 4)] = other[yh, which, g]
            at = g * 4 + lax.rem(z0 + 2, 4)
            cache[which, at + core * 16] = across[0, which, g]
            cache[which, at + (1 - core) * 16] = other[2, which, g]
        for b in range(NB, NB + STEP - 1):
            cache[which, b] = jnp.zeros((ROWS, HD), jnp.bfloat16)
    starts, ends = doc_bounds(doc_ids)
    for h in range(HEADS):
        flat[h * ROWS : (h + 1) * ROWS, :] = queries[:, h * HD : (h + 1) * HD]

    row = ctx * ROWS + lax.broadcasted_iota(jnp.int32, (1, ROWS), 1)
    row_start = jnp.zeros((1, ROWS), jnp.int32)
    first = jnp.int32(0)
    for d in range(1, NDOC):
        row_start = jnp.where(row >= starts[d], starts[d], row_start)
        first = jnp.where(ctx * ROWS >= starts[d], starts[d], first)
    block0 = first // ROWS
    factor = SCALE * math.log2(math.e)
    acc[...] = jnp.zeros_like(acc)

    def step(i, carry):
        old, total = carry
        at = block0 + STEP * i
        key = cache[0, pl.ds(at, STEP)].reshape(STEP * ROWS, HD)
        value = cache[1, pl.ds(at, STEP)].reshape(STEP * ROWS, HD)
        place = at * ROWS + lax.broadcasted_iota(jnp.int32, (STEP * ROWS, ROWS), 0)
        bias = jnp.where((place <= row) & (place >= row_start), 0.0, NEG)
        s = lax.dot_general(key, flat[...], (((1,), (1,)), ((), ())), preferred_element_type=jnp.float32)
        s = s * factor + jnp.concatenate([bias] * HEADS, axis=1)
        new = jnp.maximum(old, jnp.max(s, axis=0, keepdims=True))
        p = jnp.exp2(s - new)
        alpha = jnp.exp2(old - new)
        total = total * alpha + jnp.sum(p, axis=0, keepdims=True)
        acc[...] = acc[...] * alpha + lax.dot_general(
            value, p.astype(jnp.bfloat16), (((0,), (0,)), ((), ())), preferred_element_type=jnp.float32
        )
        return new, total

    wide = (1, HEADS * ROWS)
    _, total = lax.fori_loop(
        0, (ctx - block0 + STEP) // STEP, step, (jnp.full(wide, NEG, jnp.float32), jnp.zeros(wide, jnp.float32))
    )
    mixed = acc[...] / total
    for h in range(HEADS):
        context[:, h * HD : (h + 1) * HD] = jnp.transpose(mixed[:, h * ROWS : (h + 1) * ROWS]).astype(jnp.bfloat16)

    asked = jnp.int32(0)
    start = jnp.int32(0)
    length = jnp.int32(0)
    for d in range(NDOC):
        mine = replica_of[d] == ctx
        asked = jnp.where(mine, 1, asked)
        start = jnp.where(mine, starts[d], start)
        length = jnp.where(mine, ends[d] - starts[d], length)

    @pl.when(asked == 0)
    def _():
        replica_keys[...] = jnp.zeros_like(replica_keys)
        replica_values[...] = jnp.zeros_like(replica_values)

    @pl.when(asked == 1)
    def _():
        offset = lax.rem(start, ROWS)
        begin = start // ROWS
        r = lax.broadcasted_iota(jnp.int32, (2 * ROWS, ROWS), 0)
        s = lax.broadcasted_iota(jnp.int32, (2 * ROWS, ROWS), 1)
        hot = (r == s + offset).astype(jnp.bfloat16)
        slot = lax.broadcasted_iota(jnp.int32, (HD // 2, ROWS), 1)
        for i in range(MOST // ROWS):
            at = jnp.minimum(begin + i, NB - 1)
            live = slot + i * ROWS < length
            for which, out in ((0, replica_keys), (1, replica_values)):
                source = cache[which, pl.ds(at, 2)].reshape(2 * ROWS, HD)
                moved = lax.dot_general(source, hot, (((0,), (0,)), ((), ())), preferred_element_type=jnp.float32)
                moved = jnp.where(core == 0, moved[: HD // 2], moved[HD // 2 :])
                out[:, i * ROWS : (i + 1) * ROWS] = jnp.where(live, moved, 0.0).astype(jnp.bfloat16)


def prefill(replica_of, doc_ids, queries, parts):
    vmem = pl.BlockSpec(memory_space=pltpu.VMEM)
    return pl.pallas_call(
        prefill_kernel,
        out_shape=(
            jax.ShapeDtypeStruct((ROWS, HEADS * HD), jnp.bfloat16),
            jax.ShapeDtypeStruct((HD // 2, MOST), jnp.bfloat16),
            jax.ShapeDtypeStruct((HD // 2, MOST), jnp.bfloat16),
        ),
        in_specs=[pl.BlockSpec(memory_space=pltpu.SMEM)] + [vmem] * 6,
        scratch_shapes=[
            pltpu.VMEM((2, NB + STEP - 1, ROWS, HD), jnp.bfloat16),
            pltpu.VMEM((HEADS * ROWS, HD), jnp.bfloat16),
            pltpu.VMEM((HD, HEADS * ROWS), jnp.float32),
        ],
        compiler_params=pltpu.CompilerParams(vmem_limit_bytes=16 * 1024 * 1024),
        cost_estimate=pl.CostEstimate(flops=2 * 10**9, bytes_accessed=4 * 10**6, transcendentals=2 * 10**6),
        name="prefill",
    )(replica_of, doc_ids, queries, *parts)


def from_sides(a, by):
    pairs = []
    for yh in range(2):
        for z in range(16):
            for t in range(16):
                core = t % 2
                source = (z + (by if core == 0 else -by)) % 16
                pairs.append(((yh * 16 + source) * 16 + t, (yh * 16 + z) * 16 + t))
    return lax.ppermute(a, CTX + TP, pairs)


def local(queries, keys, values, doc_ids, replica_of, step_query, step_key, step_value, out_weight):
    half = lax.all_to_all(pick(keys, values, 4), "z1", 0, 0)
    far = lax.all_gather(half, ("yh", "c"), axis=0).reshape(2, 2, 4, ROWS, HD)
    near = from_sides(far, 1)
    across = from_sides(lax.dynamic_slice_in_dim(far, lax.axis_index("c"), 1, 0), 2)
    both = jnp.concatenate(lax.optimization_barrier((near, across)), axis=0)
    other = lax.ppermute(both, "c", [(0, 1), (1, 0)])
    parts = [far, near, across, other]
    blocks = doc_ids.reshape(NB, ROWS)
    terms = decode(blocks, step_query, step_key, step_value, out_weight, parts)
    summed = lax.all_to_all(terms, TP, 0, 0)
    context, replica_keys, replica_values = prefill(replica_of, blocks, queries, parts)
    hot = (replica_of[None, :] == jnp.arange(NB, dtype=jnp.int32)[:, None]).astype(jnp.float32)
    projected = jnp.sum(summed.astype(jnp.float32), axis=0)
    next_hidden = jnp.sum(hot[:, :, None] * projected[None, :NDOC], axis=1).astype(jnp.bfloat16)
    return (context, next_hidden, replica_keys[None], replica_values[None])


def solution(mesh):
    fine = Mesh(np.asarray(mesh.devices).reshape(2, 4, 4, 4, 2, 2), CTX + TP)
    placed = (
        P(CTX, TP),
        P(CTX, None),
        P(CTX, None),
        P(),
        P(),
        P(None, TP),
        P(),
        P(),
        P(TP, CTX),
    )
    return jax.shard_map(
        local,
        mesh=fine,
        in_specs=placed,
        out_specs=(P(CTX, TP), P(None, CTX), P(CTX, TP, None), P(CTX, TP, None)),
        check_vma=False,
    )
```

```python
import math

import jax
import jax.numpy as jnp
import numpy as np
from jax import lax
from jax.experimental import pallas as pl
from jax.experimental.pallas import tpu as pltpu
from jax.sharding import Mesh
from jax.sharding import PartitionSpec as P

H = 96
KVH = 8
HD = 128
NDOC = 4
ROWS = 128
NB = 32
MOST = 2560
HEADS = 6
SCALE = 1.0 / math.sqrt(HD)
CTX = ("yh", "z1", "z0")
TP = ("x", "yl", "c")
NEG = -1e30


def position():
    z0 = lax.axis_index("z0")
    ctx = lax.axis_index("yh") * 16 + lax.axis_index("z1") * 4 + z0
    return ctx, lax.axis_index("c"), lax.axis_index("x") * 2 + lax.axis_index("yl"), z0


def pick_kernel(keys, values, out, sem):
    _, core, head, _ = position()
    columns = pl.ds(pl.multiple_of(head * HD, HD), HD)
    for which, source in ((0, keys), (1, values)):

        @pl.when(core == which)
        def _():
            copy = pltpu.make_async_copy(source.at[:, columns], out, sem)
            copy.start()
            copy.wait()


def pick(keys, values):
    return pl.pallas_call(
        pick_kernel,
        out_shape=jax.ShapeDtypeStruct((ROWS, HD), jnp.bfloat16),
        in_specs=[pl.BlockSpec(memory_space=pltpu.HBM)] * 2,
        out_specs=pl.BlockSpec(memory_space=pltpu.VMEM),
        scratch_shapes=[pltpu.SemaphoreType.DMA],
        compiler_params=pltpu.CompilerParams(vmem_limit_bytes=60 * 1024 * 1024),
        name="pick",
    )(keys, values)


def doc_bounds(doc_ids):
    ids = doc_ids[...]
    starts = [jnp.int32(0)] + [jnp.sum((ids < d).astype(jnp.int32)) for d in range(1, NDOC)]
    return starts, starts[1:] + [jnp.int32(NB * ROWS)]


ROW = HEADS * NDOC
PAD = 32


def decode_kernel(
    doc_ids, step_query, step_key, step_value, weight, far, near, across, other, terms, query, own_key, own_value
):
    _, core, head, z0 = position()
    columns = pl.ds(pl.multiple_of(head * HD, HD), HD)
    side = 1 - 2 * core
    starts, ends = doc_bounds(doc_ids)
    steps = step_query[...].astype(jnp.float32)
    step_keys = step_key[:, columns].astype(jnp.float32)
    step_values = step_value[:, columns].astype(jnp.float32)
    for ref in (query, own_key, own_value):
        ref[ROW:PAD, :] = jnp.zeros((PAD - ROW, HD), jnp.float32)
    for h in range(HEADS):
        rows = slice(h * NDOC, (h + 1) * NDOC)
        query[rows, :] = steps[:, h * HD : (h + 1) * HD]
        own_key[rows, :] = step_keys
        own_value[rows, :] = step_values
    q = query[...]
    document = lax.broadcasted_iota(jnp.int32, (PAD, 1), 0) % NDOC
    low = jnp.zeros((PAD, 1), jnp.int32)
    high = jnp.zeros((PAD, 1), jnp.int32)
    for d in range(NDOC):
        low = jnp.where(document == d, starts[d], low)
        high = jnp.where(document == d, ends[d], high)
    narrow = q.astype(jnp.bfloat16)
    groups = [(far, 0, z0, 0), (far, 1, z0, 1), (near, 0, z0 + 4 + side, 0), (near, 1, z0 + 4 + side, 1)]
    groups += [(other, 0, z0 + 4 - side, 0), (other, 1, z0 + 4 - side, 1), (across, 0, z0 + 2, core), (other, 2, z0 + 2, 1 - core)]
    at = lax.broadcasted_iota(jnp.int32, (1, 4 * ROWS), 1)
    at = at // ROWS * (4 * ROWS) + at % ROWS
    nums, tops = [], []
    for ref, index, kind, yh in groups:
        place = at + (yh * (16 * ROWS) + lax.rem(kind, 4) * ROWS)
        keys = ref[index, 0].reshape(4 * ROWS, HD)
        s = lax.dot_general(narrow, keys, (((1,), (1,)), ((), ())), preferred_element_type=jnp.float32)
        s = jnp.where((place >= low) & (place < high), s * SCALE, NEG)
        nums.append(s)
        tops.append(jnp.max(s, axis=1, keepdims=True))
    own_score = jnp.sum(q * own_key[...], axis=1, keepdims=True) * SCALE
    top = own_score
    for t in tops:
        top = jnp.maximum(top, t)
    own_prob = jnp.exp(own_score - top)
    total = own_prob
    mixed = own_prob.astype(jnp.bfloat16).astype(jnp.float32) * own_value[...]
    for s, (ref, index, _, _) in zip(nums, groups):
        p = jnp.exp(s - top)
        total = total + jnp.sum(p, axis=1, keepdims=True)
        values = ref[index, 1].reshape(4 * ROWS, HD)
        mixed = mixed + jnp.dot(p.astype(jnp.bfloat16), values, preferred_element_type=jnp.float32)
    query[...] = mixed / total
    wide = jnp.concatenate([query[h * NDOC : (h + 1) * NDOC, :] for h in range(HEADS)], axis=1)
    wide = jnp.concatenate([wide, jnp.zeros_like(wide)], axis=0)
    term = jnp.dot(wide.astype(jnp.bfloat16), weight[...], preferred_element_type=jnp.float32).astype(terms.dtype)
    for k in range(16):
        terms[k] = term


def decode(doc_ids, step_query, step_key, step_value, weight, parts):
    return pl.pallas_call(
        decode_kernel,
        out_shape=jax.ShapeDtypeStruct((16, 8, weight.shape[1]), jnp.bfloat16),
        scratch_shapes=[pltpu.VMEM((PAD, HD), jnp.float32)] * 3,
        compiler_params=pltpu.CompilerParams(vmem_limit_bytes=12 * 1024 * 1024),
        cost_estimate=pl.CostEstimate(flops=10**8, bytes_accessed=4 * 10**6, transcendentals=2 * 10**5),
        name="decode",
    )(doc_ids, step_query, step_key, step_value, weight, *parts)


STEP = 4


def prefill_kernel(
    replica_of, doc_ids, queries, far, near, across, other,
    context, replica_keys, replica_values,
    cache, flat, acc,
):
    ctx, core, _, z0 = position()
    side = 1 - 2 * core
    for which in range(2):
        for g in range(4):
            for yh in range(2):
                at = yh * 16 + g * 4
                cache[which, at + z0] = far[yh, which, g]
                cache[which, at + lax.rem(z0 + 4 + side, 4)] = near[yh, which, g]
                cache[which, at + lax.rem(z0 + 4 - side, 4)] = other[yh, which, g]
            at = g * 4 + lax.rem(z0 + 2, 4)
            cache[which, at + core * 16] = across[0, which, g]
            cache[which, at + (1 - core) * 16] = other[2, which, g]
        for b in range(NB, NB + STEP - 1):
            cache[which, b] = jnp.zeros((ROWS, HD), jnp.bfloat16)
    starts, ends = doc_bounds(doc_ids)
    for h in range(HEADS):
        flat[h * ROWS : (h + 1) * ROWS, :] = queries[:, h * HD : (h + 1) * HD]

    row = ctx * ROWS + lax.broadcasted_iota(jnp.int32, (1, ROWS), 1)
    row_start = jnp.zeros((1, ROWS), jnp.int32)
    first = jnp.int32(0)
    for d in range(1, NDOC):
        row_start = jnp.where(row >= starts[d], starts[d], row_start)
        first = jnp.where(ctx * ROWS >= starts[d], starts[d], first)
    block0 = first // ROWS
    factor = SCALE * math.log2(math.e)
    acc[...] = jnp.zeros_like(acc)

    def step(i, carry):
        old, total = carry
        at = block0 + STEP * i
        key = cache[0, pl.ds(at, STEP)].reshape(STEP * ROWS, HD)
        value = cache[1, pl.ds(at, STEP)].reshape(STEP * ROWS, HD)
        place = at * ROWS + lax.broadcasted_iota(jnp.int32, (STEP * ROWS, ROWS), 0)
        bias = jnp.where((place <= row) & (place >= row_start), 0.0, NEG)
        s = lax.dot_general(key, flat[...], (((1,), (1,)), ((), ())), preferred_element_type=jnp.float32)
        s = s * factor + jnp.concatenate([bias] * HEADS, axis=1)
        new = jnp.maximum(old, jnp.max(s, axis=0, keepdims=True))
        p = jnp.exp2(s - new)
        alpha = jnp.exp2(old - new)
        total = total * alpha + jnp.sum(p, axis=0, keepdims=True)
        acc[...] = acc[...] * alpha + lax.dot_general(
            value, p.astype(jnp.bfloat16), (((0,), (0,)), ((), ())), preferred_element_type=jnp.float32
        )
        return new, total

    wide = (1, HEADS * ROWS)
    _, total = lax.fori_loop(
        0, (ctx - block0 + STEP) // STEP, step, (jnp.full(wide, NEG, jnp.float32), jnp.zeros(wide, jnp.float32))
    )
    mixed = acc[...] / total
    for h in range(HEADS):
        context[:, h * HD : (h + 1) * HD] = jnp.transpose(mixed[:, h * ROWS : (h + 1) * ROWS]).astype(jnp.bfloat16)

    asked = jnp.int32(0)
    start = jnp.int32(0)
    length = jnp.int32(0)
    for d in range(NDOC):
        mine = replica_of[d] == ctx
        asked = jnp.where(mine, 1, asked)
        start = jnp.where(mine, starts[d], start)
        length = jnp.where(mine, ends[d] - starts[d], length)

    @pl.when(asked == 0)
    def _():
        replica_keys[...] = jnp.zeros_like(replica_keys)
        replica_values[...] = jnp.zeros_like(replica_values)

    @pl.when(asked == 1)
    def _():
        offset = lax.rem(start, ROWS)
        begin = start // ROWS
        r = lax.broadcasted_iota(jnp.int32, (2 * ROWS, ROWS), 0)
        s = lax.broadcasted_iota(jnp.int32, (2 * ROWS, ROWS), 1)
        hot = (r == s + offset).astype(jnp.bfloat16)
        slot = lax.broadcasted_iota(jnp.int32, (HD // 2, ROWS), 1)
        for i in range(MOST // ROWS):
            at = jnp.minimum(begin + i, NB - 1)
            live = slot + i * ROWS < length
            for which, out in ((0, replica_keys), (1, replica_values)):
                source = cache[which, pl.ds(at, 2)].reshape(2 * ROWS, HD)
                moved = lax.dot_general(source, hot, (((0,), (0,)), ((), ())), preferred_element_type=jnp.float32)
                moved = jnp.where(core == 0, moved[: HD // 2], moved[HD // 2 :])
                out[:, i * ROWS : (i + 1) * ROWS] = jnp.where(live, moved, 0.0).astype(jnp.bfloat16)


def prefill(replica_of, doc_ids, queries, parts):
    vmem = pl.BlockSpec(memory_space=pltpu.VMEM)
    return pl.pallas_call(
        prefill_kernel,
        out_shape=(
            jax.ShapeDtypeStruct((ROWS, HEADS * HD), jnp.bfloat16),
            jax.ShapeDtypeStruct((HD // 2, MOST), jnp.bfloat16),
            jax.ShapeDtypeStruct((HD // 2, MOST), jnp.bfloat16),
        ),
        in_specs=[pl.BlockSpec(memory_space=pltpu.SMEM)] + [vmem] * 6,
        scratch_shapes=[
            pltpu.VMEM((2, NB + STEP - 1, ROWS, HD), jnp.bfloat16),
            pltpu.VMEM((HEADS * ROWS, HD), jnp.bfloat16),
            pltpu.VMEM((HD, HEADS * ROWS), jnp.float32),
        ],
        compiler_params=pltpu.CompilerParams(vmem_limit_bytes=16 * 1024 * 1024),
        cost_estimate=pl.CostEstimate(flops=2 * 10**9, bytes_accessed=4 * 10**6, transcendentals=2 * 10**6),
        name="prefill",
    )(replica_of, doc_ids, queries, *parts)


def from_sides(a, by):
    pairs = []
    for yh in range(2):
        for z in range(16):
            for t in range(16):
                core = t % 2
                source = (z + (by if core == 0 else -by)) % 16
                pairs.append(((yh * 16 + source) * 16 + t, (yh * 16 + z) * 16 + t))
    return lax.ppermute(a, CTX + TP, pairs)


def local(queries, keys, values, doc_ids, replica_of, step_query, step_key, step_value, out_weight):
    half = lax.all_gather(pick(keys, values), "z1", axis=0)
    far = lax.all_gather(half, ("yh", "c"), axis=0).reshape(2, 2, 4, ROWS, HD)
    near = from_sides(far, 1)
    across = from_sides(lax.dynamic_slice_in_dim(far, lax.axis_index("c"), 1, 0), 2)
    both = jnp.concatenate(lax.optimization_barrier((near, across)), axis=0)
    other = lax.ppermute(both, "c", [(0, 1), (1, 0)])
    parts = [far, near, across, other]
    blocks = doc_ids.reshape(NB, ROWS)
    terms = decode(blocks, step_query, step_key, step_value, out_weight, parts)
    summed = lax.all_to_all(terms, TP, 0, 0)
    context, replica_keys, replica_values = prefill(replica_of, blocks, queries, parts)
    hot = (replica_of[None, :] == jnp.arange(NB, dtype=jnp.int32)[:, None]).astype(jnp.float32)
    projected = jnp.sum(summed.astype(jnp.float32), axis=0)
    next_hidden = jnp.sum(hot[:, :, None] * projected[None, :NDOC], axis=1).astype(jnp.bfloat16)
    return (context, next_hidden, replica_keys[None], replica_values[None])


def solution(mesh):
    fine = Mesh(np.asarray(mesh.devices).reshape(2, 4, 4, 4, 2, 2), CTX + TP)
    placed = (
        P(CTX, TP),
        P(CTX, None),
        P(CTX, None),
        P(),
        P(),
        P(None, TP),
        P(),
        P(),
        P(TP, CTX),
    )
    return jax.shard_map(
        local,
        mesh=fine,
        in_specs=placed,
        out_specs=(P(CTX, TP), P(None, CTX), P(CTX, TP, None), P(CTX, TP, None)),
        check_vma=False,
    )
```

```python
import math

import jax
import jax.numpy as jnp
import numpy as np
from jax import lax
from jax.experimental import pallas as pl
from jax.experimental.pallas import tpu as pltpu
from jax.sharding import Mesh
from jax.sharding import PartitionSpec as P

H = 96
KVH = 8
HD = 128
NDOC = 4
ROWS = 128
NB = 32
MOST = 2560
HEADS = 6
SCALE = 1.0 / math.sqrt(HD)
CTX = ("yh", "z1", "z0")
TP = ("x", "yl", "c")
NEG = -1e30


def position():
    z0 = lax.axis_index("z0")
    ctx = lax.axis_index("yh") * 16 + lax.axis_index("z1") * 4 + z0
    return ctx, lax.axis_index("c"), lax.axis_index("x") * 2 + lax.axis_index("yl"), z0


def pick_kernel(keys, values, out, sem):
    _, core, head, _ = position()
    columns = pl.ds(pl.multiple_of(head * HD, HD), HD)
    for which, source in ((0, keys), (1, values)):

        @pl.when(core == which)
        def _():
            copy = pltpu.make_async_copy(source.at[:, columns], out, sem)
            copy.start()
            copy.wait()


def pick(keys, values):
    return pl.pallas_call(
        pick_kernel,
        out_shape=jax.ShapeDtypeStruct((ROWS, HD), jnp.bfloat16),
        in_specs=[pl.BlockSpec(memory_space=pltpu.HBM)] * 2,
        out_specs=pl.BlockSpec(memory_space=pltpu.VMEM),
        scratch_shapes=[pltpu.SemaphoreType.DMA],
        compiler_params=pltpu.CompilerParams(vmem_limit_bytes=60 * 1024 * 1024),
        name="pick",
    )(keys, values)


def doc_bounds(doc_ids):
    ids = doc_ids[...]
    starts = [jnp.int32(0)] + [jnp.sum((ids < d).astype(jnp.int32)) for d in range(1, NDOC)]
    return starts, starts[1:] + [jnp.int32(NB * ROWS)]


ROW = HEADS * NDOC
PAD = 32


def combine(parts):
    top = parts[0][1]
    for _, weight in parts[1:]:
        top = jnp.maximum(top, weight)
    shares = [jnp.exp(weight - top) for _, weight in parts]
    return sum(share * mixed for share, (mixed, _) in zip(shares, parts)) / sum(shares)


def class_part_kernel(doc_ids, step_query, far, out, query):
    z0 = position()[3]
    query[...] = jnp.zeros_like(query)
    steps = step_query[...].astype(jnp.float32)
    for h in range(HEADS):
        query[h * NDOC : (h + 1) * NDOC, :] = steps[:, h * HD : (h + 1) * HD]
    narrow = query[...].astype(jnp.bfloat16)
    starts, ends = doc_bounds(doc_ids)
    document = lax.broadcasted_iota(jnp.int32, (PAD, 1), 0) % NDOC
    low = jnp.zeros((PAD, 1), jnp.int32)
    high = jnp.zeros((PAD, 1), jnp.int32)
    for d in range(NDOC):
        low = jnp.where(document == d, starts[d], low)
        high = jnp.where(document == d, ends[d], high)
    at = lax.broadcasted_iota(jnp.int32, (1, 4 * ROWS), 1)
    at = at // ROWS * (4 * ROWS) + at % ROWS + z0 * ROWS
    scores, seen = [], []
    top = jnp.full((PAD, 1), NEG, jnp.float32)
    for yh in range(2):
        place = at + yh * (16 * ROWS)
        mask = (place >= low) & (place < high)
        keys = far[yh, 0].reshape(4 * ROWS, HD)
        s = lax.dot_general(narrow, keys, (((1,), (1,)), ((), ())), preferred_element_type=jnp.float32)
        s = jnp.where(mask, s * SCALE, NEG)
        top = jnp.maximum(top, jnp.max(s, axis=1, keepdims=True))
        scores.append(s)
        seen.append(mask)
    total = jnp.zeros((PAD, 1), jnp.float32)
    mixed = jnp.zeros((PAD, HD), jnp.float32)
    for yh in range(2):
        p = jnp.where(seen[yh], jnp.exp(scores[yh] - top), 0.0)
        total = total + jnp.sum(p, axis=1, keepdims=True)
        values = far[yh, 1].reshape(4 * ROWS, HD)
        mixed = mixed + jnp.dot(p.astype(jnp.bfloat16), values, preferred_element_type=jnp.float32)
    some = total > 0.0
    safe = jnp.where(some, total, 1.0)
    weight = jnp.where(some, top + jnp.log(safe), NEG)
    sub = lax.broadcasted_iota(jnp.int32, (PAD, HD), 0)
    lane = lax.broadcasted_iota(jnp.int32, (PAD, HD), 1)
    line = jnp.sum(jnp.where(sub == lane, weight, 0.0), axis=0, keepdims=True)
    out[...] = jnp.where(sub == ROW, line, mixed / safe)


def class_part(doc_ids, step_query, far):
    return pl.pallas_call(
        class_part_kernel,
        out_shape=jax.ShapeDtypeStruct((PAD, HD), jnp.float32),
        scratch_shapes=[pltpu.VMEM((PAD, HD), jnp.float32)],
        compiler_params=pltpu.CompilerParams(vmem_limit_bytes=8 * 1024 * 1024),
        cost_estimate=pl.CostEstimate(flops=3 * 10**7, bytes_accessed=10**6, transcendentals=4 * 10**4),
        name="class_part",
    )(doc_ids, step_query, far)


def project_kernel(parts, step_query, step_key, step_value, weight, terms, product, mixed):
    head = position()[2]
    columns = pl.ds(pl.multiple_of(head * HD, HD), HD)
    steps = step_query[...].astype(jnp.float32)
    step_keys = step_key[:, columns].astype(jnp.float32)
    step_values = step_value[:, columns].astype(jnp.float32)
    for ref in (product, mixed):
        ref[ROW:PAD, :] = jnp.zeros((PAD - ROW, HD), jnp.float32)
    for h in range(HEADS):
        rows = slice(h * NDOC, (h + 1) * NDOC)
        product[rows, :] = steps[:, h * HD : (h + 1) * HD] * step_keys
        mixed[rows, :] = step_values
    sub = lax.broadcasted_iota(jnp.int32, (PAD, HD), 0)
    lane = lax.broadcasted_iota(jnp.int32, (PAD, HD), 1)
    found = [(mixed[...], jnp.sum(product[...], axis=1, keepdims=True) * SCALE)]
    for k in range(parts.shape[0]):
        part = parts[k]
        line = jnp.sum(jnp.where(sub == ROW, part, 0.0), axis=0, keepdims=True)
        found.append((part, jnp.sum(jnp.where(sub == lane, line, 0.0), axis=1, keepdims=True)))
    mixed[...] = combine(found)
    wide = jnp.concatenate([mixed[h * NDOC : (h + 1) * NDOC, :] for h in range(HEADS)], axis=1)
    wide = jnp.concatenate([wide, jnp.zeros_like(wide)], axis=0)
    term = jnp.dot(wide.astype(jnp.bfloat16), weight[...], preferred_element_type=jnp.float32).astype(terms.dtype)
    for k in range(16):
        terms[k] = term


def project(parts, step_query, step_key, step_value, weight):
    return pl.pallas_call(
        project_kernel,
        out_shape=jax.ShapeDtypeStruct((16, 8, weight.shape[1]), jnp.bfloat16),
        scratch_shapes=[pltpu.VMEM((PAD, HD), jnp.float32)] * 2,
        compiler_params=pltpu.CompilerParams(vmem_limit_bytes=8 * 1024 * 1024),
        cost_estimate=pl.CostEstimate(flops=10**7, bytes_accessed=10**6, transcendentals=10**3),
        name="project",
    )(parts, step_query, step_key, step_value, weight)


STEP = 4


def prefill_kernel(
    replica_of, doc_ids, queries, far, near, across, other,
    context, replica_keys, replica_values, hot,
    cache, flat, acc,
):
    ctx, core, _, z0 = position()
    side = 1 - 2 * core
    for which in range(2):
        for g in range(4):
            for yh in range(2):
                at = yh * 16 + g * 4
                cache[which, at + z0] = far[yh, which, g]
                cache[which, at + lax.rem(z0 + 4 + side, 4)] = near[yh, which, g]
                cache[which, at + lax.rem(z0 + 4 - side, 4)] = other[yh, which, g]
            at = g * 4 + lax.rem(z0 + 2, 4)
            cache[which, at + core * 16] = across[0, which, g]
            cache[which, at + (1 - core) * 16] = other[2, which, g]
        for b in range(NB, NB + STEP - 1):
            cache[which, b] = jnp.zeros((ROWS, HD), jnp.bfloat16)
    starts, ends = doc_bounds(doc_ids)
    for h in range(HEADS):
        flat[h * ROWS : (h + 1) * ROWS, :] = queries[:, h * HD : (h + 1) * HD]

    row = ctx * ROWS + lax.broadcasted_iota(jnp.int32, (1, ROWS), 1)
    row_start = jnp.zeros((1, ROWS), jnp.int32)
    first = jnp.int32(0)
    for d in range(1, NDOC):
        row_start = jnp.where(row >= starts[d], starts[d], row_start)
        first = jnp.where(ctx * ROWS >= starts[d], starts[d], first)
    block0 = first // ROWS
    factor = SCALE * math.log2(math.e)
    acc[...] = jnp.zeros_like(acc)

    def step(i, carry):
        old, total = carry
        at = block0 + STEP * i
        key = cache[0, pl.ds(at, STEP)].reshape(STEP * ROWS, HD)
        value = cache[1, pl.ds(at, STEP)].reshape(STEP * ROWS, HD)
        place = at * ROWS + lax.broadcasted_iota(jnp.int32, (STEP * ROWS, ROWS), 0)
        bias = jnp.where((place <= row) & (place >= row_start), 0.0, NEG)
        s = lax.dot_general(key, flat[...], (((1,), (1,)), ((), ())), preferred_element_type=jnp.float32)
        s = s * factor + jnp.concatenate([bias] * HEADS, axis=1)
        new = jnp.maximum(old, jnp.max(s, axis=0, keepdims=True))
        p = jnp.exp2(s - new)
        alpha = jnp.exp2(old - new)
        total = total * alpha + jnp.sum(p, axis=0, keepdims=True)
        acc[...] = acc[...] * alpha + lax.dot_general(
            value, p.astype(jnp.bfloat16), (((0,), (0,)), ((), ())), preferred_element_type=jnp.float32
        )
        return new, total

    wide = (1, HEADS * ROWS)
    _, total = lax.fori_loop(
        0, (ctx - block0 + STEP) // STEP, step, (jnp.full(wide, NEG, jnp.float32), jnp.zeros(wide, jnp.float32))
    )
    mixed = acc[...] / total
    for h in range(HEADS):
        context[:, h * HD : (h + 1) * HD] = jnp.transpose(mixed[:, h * ROWS : (h + 1) * ROWS]).astype(jnp.bfloat16)

    replica = lax.broadcasted_iota(jnp.int32, hot.shape, 0)
    document = lax.broadcasted_iota(jnp.int32, hot.shape, 1) % 8
    found = jnp.zeros(hot.shape, jnp.float32)
    for d in range(NDOC):
        found = jnp.where((document == d) & (replica == replica_of[d]), 1.0, found)
    hot[...] = found.astype(hot.dtype)

    asked = jnp.int32(0)
    start = jnp.int32(0)
    length = jnp.int32(0)
    for d in range(NDOC):
        mine = replica_of[d] == ctx
        asked = jnp.where(mine, 1, asked)
        start = jnp.where(mine, starts[d], start)
        length = jnp.where(mine, ends[d] - starts[d], length)

    @pl.when(asked == 0)
    def _():
        replica_keys[...] = jnp.zeros_like(replica_keys)
        replica_values[...] = jnp.zeros_like(replica_values)

    @pl.when(asked == 1)
    def _():
        offset = lax.rem(start, ROWS)
        begin = start // ROWS
        r = lax.broadcasted_iota(jnp.int32, (2 * ROWS, ROWS), 0)
        s = lax.broadcasted_iota(jnp.int32, (2 * ROWS, ROWS), 1)
        hot = (r == s + offset).astype(jnp.bfloat16)
        slot = lax.broadcasted_iota(jnp.int32, (HD // 2, ROWS), 1)
        for i in range(MOST // ROWS):
            at = jnp.minimum(begin + i, NB - 1)
            live = slot + i * ROWS < length
            for which, out in ((0, replica_keys), (1, replica_values)):
                source = cache[which, pl.ds(at, 2)].reshape(2 * ROWS, HD)
                moved = lax.dot_general(source, hot, (((0,), (0,)), ((), ())), preferred_element_type=jnp.float32)
                moved = jnp.where(core == 0, moved[: HD // 2], moved[HD // 2 :])
                out[:, i * ROWS : (i + 1) * ROWS] = jnp.where(live, moved, 0.0).astype(jnp.bfloat16)


def prefill(replica_of, doc_ids, queries, parts):
    vmem = pl.BlockSpec(memory_space=pltpu.VMEM)
    return pl.pallas_call(
        prefill_kernel,
        out_shape=(
            jax.ShapeDtypeStruct((ROWS, HEADS * HD), jnp.bfloat16),
            jax.ShapeDtypeStruct((HD // 2, MOST), jnp.bfloat16),
            jax.ShapeDtypeStruct((HD // 2, MOST), jnp.bfloat16),
            jax.ShapeDtypeStruct((NB, 16 * 8), jnp.bfloat16),
        ),
        in_specs=[pl.BlockSpec(memory_space=pltpu.SMEM)] + [vmem] * 6,
        scratch_shapes=[
            pltpu.VMEM((2, NB + STEP - 1, ROWS, HD), jnp.bfloat16),
            pltpu.VMEM((HEADS * ROWS, HD), jnp.bfloat16),
            pltpu.VMEM((HD, HEADS * ROWS), jnp.float32),
        ],
        compiler_params=pltpu.CompilerParams(vmem_limit_bytes=16 * 1024 * 1024),
        cost_estimate=pl.CostEstimate(flops=10**6, bytes_accessed=10**5, transcendentals=10**3),
        name="prefill",
    )(replica_of, doc_ids, queries, *parts)


def from_sides(a, by):
    pairs = []
    for yh in range(2):
        for z in range(16):
            for t in range(16):
                core = t % 2
                source = (z + (by if core == 0 else -by)) % 16
                pairs.append(((yh * 16 + source) * 16 + t, (yh * 16 + z) * 16 + t))
    return lax.ppermute(a, CTX + TP, pairs)


def local(queries, keys, values, doc_ids, replica_of, step_query, step_key, step_value, out_weight):
    half = lax.all_gather(pick(keys, values), "z1", axis=0)
    far = lax.all_gather(half, ("yh", "c"), axis=0).reshape(2, 2, 4, ROWS, HD)
    near = from_sides(far, 1)
    across = from_sides(lax.dynamic_slice_in_dim(far, lax.axis_index("c"), 1, 0), 2)
    blocks = doc_ids.reshape(NB, ROWS)
    decoded = lax.all_to_all(jnp.broadcast_to(class_part(blocks, step_query, far)[None], (4, PAD, HD)), "z0", 0, 0)
    terms = project(decoded, step_query, step_key, step_value, out_weight)
    near, across, terms = lax.optimization_barrier((near, across, terms))
    both = jnp.concatenate((near, across), axis=0)
    other = lax.ppermute(both, "c", [(0, 1), (1, 0)])
    parts = [far, near, across, other]
    summed = lax.all_to_all(terms, TP, 0, 0)
    context, replica_keys, replica_values, hot = prefill(replica_of, blocks, queries, parts)
    next_hidden = jnp.dot(hot, summed.reshape(16 * 8, -1), preferred_element_type=jnp.float32).astype(jnp.bfloat16)
    return (context, next_hidden, replica_keys[None], replica_values[None])


def solution(mesh):
    fine = Mesh(np.asarray(mesh.devices).reshape(2, 4, 4, 4, 2, 2), CTX + TP)
    placed = (
        P(CTX, TP),
        P(CTX, None),
        P(CTX, None),
        P(),
        P(),
        P(None, TP),
        P(),
        P(),
        P(TP, CTX),
    )
    return jax.shard_map(
        local,
        mesh=fine,
        in_specs=placed,
        out_specs=(P(CTX, TP), P(None, CTX), P(CTX, TP, None), P(CTX, TP, None)),
        check_vma=False,
    )
```

```python
import math

import jax
import jax.numpy as jnp
import numpy as np
from jax import lax
from jax.experimental import pallas as pl
from jax.experimental.pallas import tpu as pltpu
from jax.sharding import Mesh
from jax.sharding import PartitionSpec as P

H = 96
KVH = 8
HD = 128
NDOC = 4
ROWS = 128
NB = 32
MOST = 2560
HEADS = 6
SCALE = 1.0 / math.sqrt(HD)
CTX = ("yh", "z1", "z0")
TP = ("x", "yl", "c")
NEG = -1e30


def position():
    z0 = lax.axis_index("z0")
    ctx = lax.axis_index("yh") * 16 + lax.axis_index("z1") * 4 + z0
    return ctx, lax.axis_index("c"), lax.axis_index("x") * 2 + lax.axis_index("yl"), z0


def pick_kernel(keys, values, out, sem):
    _, core, head, _ = position()
    columns = pl.ds(pl.multiple_of(head * HD, HD), HD)
    for which, source in ((0, keys), (1, values)):

        @pl.when(core == which)
        def _():
            copy = pltpu.make_async_copy(source.at[:, columns], out, sem)
            copy.start()
            copy.wait()


def pick(keys, values):
    return pl.pallas_call(
        pick_kernel,
        out_shape=jax.ShapeDtypeStruct((ROWS, HD), jnp.bfloat16),
        in_specs=[pl.BlockSpec(memory_space=pltpu.HBM)] * 2,
        out_specs=pl.BlockSpec(memory_space=pltpu.VMEM),
        scratch_shapes=[pltpu.SemaphoreType.DMA],
        compiler_params=pltpu.CompilerParams(vmem_limit_bytes=60 * 1024 * 1024),
        name="pick",
    )(keys, values)


def doc_bounds(doc_ids):
    ids = doc_ids[...]
    starts = [jnp.int32(0)] + [jnp.sum((ids < d).astype(jnp.int32)) for d in range(1, NDOC)]
    return starts, starts[1:] + [jnp.int32(NB * ROWS)]


ROW = HEADS * NDOC
PAD = 32


def combine(parts):
    top = parts[0][1]
    for _, weight in parts[1:]:
        top = jnp.maximum(top, weight)
    shares = [jnp.exp(weight - top) for _, weight in parts]
    return sum(share * mixed for share, (mixed, _) in zip(shares, parts)) / sum(shares)


def class_part_kernel(doc_ids, step_query, far, out, query):
    z0 = position()[3]
    query[...] = jnp.zeros_like(query)
    steps = step_query[...].astype(jnp.float32)
    for h in range(HEADS):
        query[h * NDOC : (h + 1) * NDOC, :] = steps[:, h * HD : (h + 1) * HD]
    narrow = query[...].astype(jnp.bfloat16)
    starts, ends = doc_bounds(doc_ids)
    document = lax.broadcasted_iota(jnp.int32, (PAD, 1), 0) % NDOC
    low = jnp.zeros((PAD, 1), jnp.int32)
    high = jnp.zeros((PAD, 1), jnp.int32)
    for d in range(NDOC):
        low = jnp.where(document == d, starts[d], low)
        high = jnp.where(document == d, ends[d], high)
    at = lax.broadcasted_iota(jnp.int32, (1, 4 * ROWS), 1)
    at = at // ROWS * (4 * ROWS) + at % ROWS + z0 * ROWS
    scores, seen = [], []
    top = jnp.full((PAD, 1), NEG, jnp.float32)
    for yh in range(2):
        place = at + yh * (16 * ROWS)
        mask = (place >= low) & (place < high)
        keys = far[yh, 0].reshape(4 * ROWS, HD)
        s = lax.dot_general(narrow, keys, (((1,), (1,)), ((), ())), preferred_element_type=jnp.float32)
        s = jnp.where(mask, s * SCALE, NEG)
        top = jnp.maximum(top, jnp.max(s, axis=1, keepdims=True))
        scores.append(s)
        seen.append(mask)
    total = jnp.zeros((PAD, 1), jnp.float32)
    mixed = jnp.zeros((PAD, HD), jnp.float32)
    for yh in range(2):
        p = jnp.where(seen[yh], jnp.exp(scores[yh] - top), 0.0)
        total = total + jnp.sum(p, axis=1, keepdims=True)
        values = far[yh, 1].reshape(4 * ROWS, HD)
        mixed = mixed + jnp.dot(p.astype(jnp.bfloat16), values, preferred_element_type=jnp.float32)
    some = total > 0.0
    safe = jnp.where(some, total, 1.0)
    weight = jnp.where(some, top + jnp.log(safe), NEG)
    sub = lax.broadcasted_iota(jnp.int32, (PAD, HD), 0)
    lane = lax.broadcasted_iota(jnp.int32, (PAD, HD), 1)
    line = jnp.sum(jnp.where(sub == lane, weight, 0.0), axis=0, keepdims=True)
    out[...] = jnp.where(sub == ROW, line, mixed / safe)


def class_part(doc_ids, step_query, far):
    return pl.pallas_call(
        class_part_kernel,
        out_shape=jax.ShapeDtypeStruct((PAD, HD), jnp.float32),
        scratch_shapes=[pltpu.VMEM((PAD, HD), jnp.float32)],
        compiler_params=pltpu.CompilerParams(vmem_limit_bytes=8 * 1024 * 1024),
        cost_estimate=pl.CostEstimate(flops=3 * 10**7, bytes_accessed=10**6, transcendentals=4 * 10**4),
        name="class_part",
    )(doc_ids, step_query, far)


def project_kernel(parts, step_query, step_key, step_value, weight, terms, product, mixed):
    head = position()[2]
    columns = pl.ds(pl.multiple_of(head * HD, HD), HD)
    steps = step_query[...].astype(jnp.float32)
    step_keys = step_key[:, columns].astype(jnp.float32)
    step_values = step_value[:, columns].astype(jnp.float32)
    for ref in (product, mixed):
        ref[ROW:PAD, :] = jnp.zeros((PAD - ROW, HD), jnp.float32)
    for h in range(HEADS):
        rows = slice(h * NDOC, (h + 1) * NDOC)
        product[rows, :] = steps[:, h * HD : (h + 1) * HD] * step_keys
        mixed[rows, :] = step_values
    sub = lax.broadcasted_iota(jnp.int32, (PAD, HD), 0)
    lane = lax.broadcasted_iota(jnp.int32, (PAD, HD), 1)
    found = [(mixed[...], jnp.sum(product[...], axis=1, keepdims=True) * SCALE)]
    for k in range(parts.shape[0]):
        part = parts[k]
        line = jnp.sum(jnp.where(sub == ROW, part, 0.0), axis=0, keepdims=True)
        found.append((part, jnp.sum(jnp.where(sub == lane, line, 0.0), axis=1, keepdims=True)))
    mixed[...] = combine(found)
    wide = jnp.concatenate([mixed[h * NDOC : (h + 1) * NDOC, :] for h in range(HEADS)], axis=1)
    wide = jnp.concatenate([wide, jnp.zeros_like(wide)], axis=0)
    term = jnp.dot(wide.astype(jnp.bfloat16), weight[...], preferred_element_type=jnp.float32).astype(terms.dtype)
    for k in range(16):
        terms[k] = term


def project(parts, step_query, step_key, step_value, weight):
    return pl.pallas_call(
        project_kernel,
        out_shape=jax.ShapeDtypeStruct((16, 8, weight.shape[1]), jnp.bfloat16),
        scratch_shapes=[pltpu.VMEM((PAD, HD), jnp.float32)] * 2,
        compiler_params=pltpu.CompilerParams(vmem_limit_bytes=8 * 1024 * 1024),
        cost_estimate=pl.CostEstimate(flops=10**7, bytes_accessed=10**6, transcendentals=10**3),
        name="project",
    )(parts, step_query, step_key, step_value, weight)


STEP = 4


def prefill_kernel(
    replica_of, doc_ids, queries, far, near, across, other0, other1,
    context, replica_keys, replica_values, hot,
    cache, flat, acc,
):
    ctx, core, _, z0 = position()
    side = 1 - 2 * core
    for which in range(2):
        for g in range(4):
            for yh in range(2):
                at = yh * 16 + g * 4
                cache[which, at + z0] = far[yh, which, g]
                cache[which, at + lax.rem(z0 + 4 + side, 4)] = near[yh, which, g]
                cache[which, at + lax.rem(z0 + 4 - side, 4)] = (other0, other1)[yh][1 - core, which, g]
                cache[which, at + lax.rem(z0 + 2, 4)] = across[yh, which, g]
        for b in range(NB, NB + STEP - 1):
            cache[which, b] = jnp.zeros((ROWS, HD), jnp.bfloat16)
    starts, ends = doc_bounds(doc_ids)
    for h in range(HEADS):
        flat[h * ROWS : (h + 1) * ROWS, :] = queries[:, h * HD : (h + 1) * HD]

    row = ctx * ROWS + lax.broadcasted_iota(jnp.int32, (1, ROWS), 1)
    row_start = jnp.zeros((1, ROWS), jnp.int32)
    first = jnp.int32(0)
    for d in range(1, NDOC):
        row_start = jnp.where(row >= starts[d], starts[d], row_start)
        first = jnp.where(ctx * ROWS >= starts[d], starts[d], first)
    block0 = first // ROWS
    factor = SCALE * math.log2(math.e)
    acc[...] = jnp.zeros_like(acc)

    def step(i, carry):
        old, total = carry
        at = block0 + STEP * i
        key = cache[0, pl.ds(at, STEP)].reshape(STEP * ROWS, HD)
        value = cache[1, pl.ds(at, STEP)].reshape(STEP * ROWS, HD)
        place = at * ROWS + lax.broadcasted_iota(jnp.int32, (STEP * ROWS, ROWS), 0)
        bias = jnp.where((place <= row) & (place >= row_start), 0.0, NEG)
        s = lax.dot_general(key, flat[...], (((1,), (1,)), ((), ())), preferred_element_type=jnp.float32)
        s = s * factor + jnp.concatenate([bias] * HEADS, axis=1)
        new = jnp.maximum(old, jnp.max(s, axis=0, keepdims=True))
        p = jnp.exp2(s - new)
        alpha = jnp.exp2(old - new)
        total = total * alpha + jnp.sum(p, axis=0, keepdims=True)
        acc[...] = acc[...] * alpha + lax.dot_general(
            value, p.astype(jnp.bfloat16), (((0,), (0,)), ((), ())), preferred_element_type=jnp.float32
        )
        return new, total

    wide = (1, HEADS * ROWS)
    _, total = lax.fori_loop(
        0, (ctx - block0 + STEP) // STEP, step, (jnp.full(wide, NEG, jnp.float32), jnp.zeros(wide, jnp.float32))
    )
    mixed = acc[...] / total
    for h in range(HEADS):
        context[:, h * HD : (h + 1) * HD] = jnp.transpose(mixed[:, h * ROWS : (h + 1) * ROWS]).astype(jnp.bfloat16)

    replica = lax.broadcasted_iota(jnp.int32, hot.shape, 0)
    document = lax.broadcasted_iota(jnp.int32, hot.shape, 1) % 8
    found = jnp.zeros(hot.shape, jnp.float32)
    for d in range(NDOC):
        found = jnp.where((document == d) & (replica == replica_of[d]), 1.0, found)
    hot[...] = found.astype(hot.dtype)

    asked = jnp.int32(0)
    start = jnp.int32(0)
    length = jnp.int32(0)
    for d in range(NDOC):
        mine = replica_of[d] == ctx
        asked = jnp.where(mine, 1, asked)
        start = jnp.where(mine, starts[d], start)
        length = jnp.where(mine, ends[d] - starts[d], length)

    @pl.when(asked == 0)
    def _():
        replica_keys[...] = jnp.zeros_like(replica_keys)
        replica_values[...] = jnp.zeros_like(replica_values)

    @pl.when(asked == 1)
    def _():
        offset = lax.rem(start, ROWS)
        begin = start // ROWS
        r = lax.broadcasted_iota(jnp.int32, (2 * ROWS, ROWS), 0)
        s = lax.broadcasted_iota(jnp.int32, (2 * ROWS, ROWS), 1)
        hot = (r == s + offset).astype(jnp.bfloat16)
        slot = lax.broadcasted_iota(jnp.int32, (HD // 2, ROWS), 1)
        for i in range(MOST // ROWS):
            at = jnp.minimum(begin + i, NB - 1)
            live = slot + i * ROWS < length
            for which, out in ((0, replica_keys), (1, replica_values)):
                source = cache[which, pl.ds(at, 2)].reshape(2 * ROWS, HD)
                moved = lax.dot_general(source, hot, (((0,), (0,)), ((), ())), preferred_element_type=jnp.float32)
                moved = jnp.where(core == 0, moved[: HD // 2], moved[HD // 2 :])
                out[:, i * ROWS : (i + 1) * ROWS] = jnp.where(live, moved, 0.0).astype(jnp.bfloat16)


def prefill(replica_of, doc_ids, queries, parts):
    vmem = pl.BlockSpec(memory_space=pltpu.VMEM)
    return pl.pallas_call(
        prefill_kernel,
        out_shape=(
            jax.ShapeDtypeStruct((ROWS, HEADS * HD), jnp.bfloat16),
            jax.ShapeDtypeStruct((HD // 2, MOST), jnp.bfloat16),
            jax.ShapeDtypeStruct((HD // 2, MOST), jnp.bfloat16),
            jax.ShapeDtypeStruct((NB, 16 * 8), jnp.bfloat16),
        ),
        in_specs=[pl.BlockSpec(memory_space=pltpu.SMEM)] + [vmem] * 7,
        scratch_shapes=[
            pltpu.VMEM((2, NB + STEP - 1, ROWS, HD), jnp.bfloat16),
            pltpu.VMEM((HEADS * ROWS, HD), jnp.bfloat16),
            pltpu.VMEM((HD, HEADS * ROWS), jnp.float32),
        ],
        compiler_params=pltpu.CompilerParams(vmem_limit_bytes=16 * 1024 * 1024),
        cost_estimate=pl.CostEstimate(flops=10**6, bytes_accessed=10**5, transcendentals=10**3),
        name="prefill",
    )(replica_of, doc_ids, queries, *parts)


def from_sides(a, by):
    pairs = []
    for yh in range(2):
        for z in range(16):
            for t in range(16):
                core = t % 2
                source = (z + (by if core == 0 else -by)) % 16
                pairs.append(((yh * 16 + source) * 16 + t, (yh * 16 + z) * 16 + t))
    return lax.ppermute(a, CTX + TP, pairs)


def local(queries, keys, values, doc_ids, replica_of, step_query, step_key, step_value, out_weight):
    half = lax.all_gather(pick(keys, values), "z1", axis=0)
    far = lax.all_gather(half, ("yh", "c"), axis=0).reshape(2, 2, 4, ROWS, HD)
    near = from_sides(far, 1)
    blocks = doc_ids.reshape(NB, ROWS)
    part = class_part(blocks, step_query, far)
    decoded = lax.all_to_all(jnp.broadcast_to(part[None], (4, PAD, HD)), "z0", 0, 0)
    across = from_sides(lax.dynamic_slice_in_dim(far, lax.axis_index("c"), 1, 0), 2)
    terms = project(decoded, step_query, step_key, step_value, out_weight)
    others = [lax.all_gather(near[yh], "c", axis=0) for yh in range(2)]
    summed = lax.all_to_all(terms, TP, 0, 0)
    across, *others = lax.optimization_barrier((across, *others))
    across, summed = lax.optimization_barrier((lax.all_gather(across[0], "c", axis=0), summed))
    parts = [far, near, across, *others]
    context, replica_keys, replica_values, hot = prefill(replica_of, blocks, queries, parts)
    next_hidden = jnp.dot(hot, summed.reshape(16 * 8, -1), preferred_element_type=jnp.float32).astype(jnp.bfloat16)
    return (context, next_hidden, replica_keys[None], replica_values[None])


def solution(mesh):
    fine = Mesh(np.asarray(mesh.devices).reshape(2, 4, 4, 4, 2, 2), CTX + TP)
    placed = (
        P(CTX, TP),
        P(CTX, None),
        P(CTX, None),
        P(),
        P(),
        P(None, TP),
        P(),
        P(),
        P(TP, CTX),
    )
    return jax.shard_map(
        local,
        mesh=fine,
        in_specs=placed,
        out_specs=(P(CTX, TP), P(None, CTX), P(CTX, TP, None), P(CTX, TP, None)),
        check_vma=False,
    )
```

```python
import math

import jax
import jax.numpy as jnp
import numpy as np
from jax import lax
from jax.experimental import pallas as pl
from jax.experimental.pallas import tpu as pltpu
from jax.sharding import Mesh
from jax.sharding import PartitionSpec as P

H = 96
KVH = 8
HD = 128
NDOC = 4
ROWS = 128
NB = 32
MOST = 2560
HEADS = 6
SCALE = 1.0 / math.sqrt(HD)
CTX = ("yh", "z1", "z0")
TP = ("x", "yl", "c")
NEG = -1e30


def position():
    z0 = lax.axis_index("z0")
    ctx = lax.axis_index("yh") * 16 + lax.axis_index("z1") * 4 + z0
    return ctx, lax.axis_index("c"), lax.axis_index("x") * 2 + lax.axis_index("yl"), z0


def pick_kernel(keys, values, out, sem):
    _, core, head, _ = position()
    columns = pl.ds(pl.multiple_of(head * HD, HD), HD)
    for which, source in ((0, keys), (1, values)):

        @pl.when(core == which)
        def _():
            copy = pltpu.make_async_copy(source.at[:, columns], out, sem)
            copy.start()
            copy.wait()


def pick(keys, values):
    return pl.pallas_call(
        pick_kernel,
        out_shape=jax.ShapeDtypeStruct((ROWS, HD), jnp.bfloat16),
        in_specs=[pl.BlockSpec(memory_space=pltpu.HBM)] * 2,
        out_specs=pl.BlockSpec(memory_space=pltpu.VMEM),
        scratch_shapes=[pltpu.SemaphoreType.DMA],
        compiler_params=pltpu.CompilerParams(vmem_limit_bytes=60 * 1024 * 1024),
        name="pick",
    )(keys, values)


def doc_bounds(doc_ids):
    ids = doc_ids[...]
    starts = [jnp.int32(0)] + [jnp.sum((ids < d).astype(jnp.int32)) for d in range(1, NDOC)]
    return starts, starts[1:] + [jnp.int32(NB * ROWS)]


ROW = HEADS * NDOC
PAD = 32


def combine(parts):
    top = parts[0][1]
    for _, weight in parts[1:]:
        top = jnp.maximum(top, weight)
    shares = [jnp.exp(weight - top) for _, weight in parts]
    return sum(share * mixed for share, (mixed, _) in zip(shares, parts)) / sum(shares)


def class_part_kernel(doc_ids, step_query, far, out, query):
    z0 = position()[3]
    query[...] = jnp.zeros_like(query)
    steps = step_query[...].astype(jnp.float32)
    for h in range(HEADS):
        query[h * NDOC : (h + 1) * NDOC, :] = steps[:, h * HD : (h + 1) * HD]
    narrow = query[...].astype(jnp.bfloat16)
    starts, ends = doc_bounds(doc_ids)
    document = lax.broadcasted_iota(jnp.int32, (PAD, 1), 0) % NDOC
    low = jnp.zeros((PAD, 1), jnp.int32)
    high = jnp.zeros((PAD, 1), jnp.int32)
    for d in range(NDOC):
        low = jnp.where(document == d, starts[d], low)
        high = jnp.where(document == d, ends[d], high)
    at = lax.broadcasted_iota(jnp.int32, (1, 4 * ROWS), 1)
    at = at // ROWS * (4 * ROWS) + at % ROWS + z0 * ROWS
    scores, seen = [], []
    top = jnp.full((PAD, 1), NEG, jnp.float32)
    for yh in range(2):
        place = at + yh * (16 * ROWS)
        mask = (place >= low) & (place < high)
        keys = far[yh, 0].reshape(4 * ROWS, HD)
        s = lax.dot_general(narrow, keys, (((1,), (1,)), ((), ())), preferred_element_type=jnp.float32)
        s = jnp.where(mask, s * SCALE, NEG)
        top = jnp.maximum(top, jnp.max(s, axis=1, keepdims=True))
        scores.append(s)
        seen.append(mask)
    total = jnp.zeros((PAD, 1), jnp.float32)
    mixed = jnp.zeros((PAD, HD), jnp.float32)
    for yh in range(2):
        p = jnp.where(seen[yh], jnp.exp(scores[yh] - top), 0.0)
        total = total + jnp.sum(p, axis=1, keepdims=True)
        values = far[yh, 1].reshape(4 * ROWS, HD)
        mixed = mixed + jnp.dot(p.astype(jnp.bfloat16), values, preferred_element_type=jnp.float32)
    some = total > 0.0
    safe = jnp.where(some, total, 1.0)
    weight = jnp.where(some, top + jnp.log(safe), NEG)
    sub = lax.broadcasted_iota(jnp.int32, (PAD, HD), 0)
    lane = lax.broadcasted_iota(jnp.int32, (PAD, HD), 1)
    line = jnp.sum(jnp.where(sub == lane, weight, 0.0), axis=0, keepdims=True)
    part = jnp.where(sub == ROW, line, mixed / safe)
    for k in range(out.shape[0]):
        out[k] = part


def class_part(doc_ids, step_query, far):
    return pl.pallas_call(
        class_part_kernel,
        out_shape=jax.ShapeDtypeStruct((4, PAD, HD), jnp.float32),
        scratch_shapes=[pltpu.VMEM((PAD, HD), jnp.float32)],
        compiler_params=pltpu.CompilerParams(vmem_limit_bytes=8 * 1024 * 1024),
        cost_estimate=pl.CostEstimate(flops=3 * 10**7, bytes_accessed=10**6, transcendentals=4 * 10**4),
        name="class_part",
    )(doc_ids, step_query, far)


def project_kernel(parts, step_query, step_key, step_value, weight, terms, product, mixed):
    head = position()[2]
    columns = pl.ds(pl.multiple_of(head * HD, HD), HD)
    steps = step_query[...].astype(jnp.float32)
    step_keys = step_key[:, columns].astype(jnp.float32)
    step_values = step_value[:, columns].astype(jnp.float32)
    for ref in (product, mixed):
        ref[ROW:PAD, :] = jnp.zeros((PAD - ROW, HD), jnp.float32)
    for h in range(HEADS):
        rows = slice(h * NDOC, (h + 1) * NDOC)
        product[rows, :] = steps[:, h * HD : (h + 1) * HD] * step_keys
        mixed[rows, :] = step_values
    sub = lax.broadcasted_iota(jnp.int32, (PAD, HD), 0)
    lane = lax.broadcasted_iota(jnp.int32, (PAD, HD), 1)
    found = [(mixed[...], jnp.sum(product[...], axis=1, keepdims=True) * SCALE)]
    for k in range(parts.shape[0]):
        part = parts[k]
        line = jnp.sum(jnp.where(sub == ROW, part, 0.0), axis=0, keepdims=True)
        found.append((part, jnp.sum(jnp.where(sub == lane, line, 0.0), axis=1, keepdims=True)))
    mixed[...] = combine(found)
    wide = jnp.concatenate([mixed[h * NDOC : (h + 1) * NDOC, :] for h in range(HEADS)], axis=1)
    wide = jnp.concatenate([wide, jnp.zeros_like(wide)], axis=0)
    term = jnp.dot(wide.astype(jnp.bfloat16), weight[...], preferred_element_type=jnp.float32).astype(terms.dtype)
    for k in range(16):
        terms[k] = term


def project(parts, step_query, step_key, step_value, weight):
    return pl.pallas_call(
        project_kernel,
        out_shape=jax.ShapeDtypeStruct((16, 8, weight.shape[1]), jnp.bfloat16),
        scratch_shapes=[pltpu.VMEM((PAD, HD), jnp.float32)] * 2,
        compiler_params=pltpu.CompilerParams(vmem_limit_bytes=8 * 1024 * 1024),
        cost_estimate=pl.CostEstimate(flops=10**7, bytes_accessed=10**6, transcendentals=10**3),
        name="project",
    )(parts, step_query, step_key, step_value, weight)


STEP = 6


def prefill_kernel(
    replica_of, doc_ids, queries, summed, far, near, across, other0, other1,
    context, next_hidden, replica_keys, replica_values,
    cache, flat, acc,
):
    ctx, core, _, z0 = position()
    side = 1 - 2 * core
    for which in range(2):
        for g in range(4):
            for yh in range(2):
                at = yh * 16 + g * 4
                cache[which, at + z0] = far[yh, which, g]
                cache[which, at + lax.rem(z0 + 4 + side, 4)] = near[yh, which, g]
                cache[which, at + lax.rem(z0 + 4 - side, 4)] = (other0, other1)[yh][1 - core, which, g]
                cache[which, at + lax.rem(z0 + 2, 4)] = across[yh, which, g]
        for b in range(NB, NB + STEP - 1):
            cache[which, b] = jnp.zeros((ROWS, HD), jnp.bfloat16)
    starts, ends = doc_bounds(doc_ids)
    for h in range(HEADS):
        flat[h * ROWS : (h + 1) * ROWS, :] = queries[:, h * HD : (h + 1) * HD]

    row = ctx * ROWS + lax.broadcasted_iota(jnp.int32, (1, ROWS), 1)
    row_start = jnp.zeros((1, ROWS), jnp.int32)
    first = jnp.int32(0)
    for d in range(1, NDOC):
        row_start = jnp.where(row >= starts[d], starts[d], row_start)
        first = jnp.where(ctx * ROWS >= starts[d], starts[d], first)
    block0 = first // ROWS
    factor = SCALE * math.log2(math.e)
    acc[...] = jnp.zeros_like(acc)

    def step(i, carry):
        old, total = carry
        at = block0 + STEP * i
        key = cache[0, pl.ds(at, STEP)].reshape(STEP * ROWS, HD)
        value = cache[1, pl.ds(at, STEP)].reshape(STEP * ROWS, HD)
        place = at * ROWS + lax.broadcasted_iota(jnp.int32, (STEP * ROWS, ROWS), 0)
        bias = jnp.where((place <= row) & (place >= row_start), 0.0, NEG)
        s = lax.dot_general(key, flat[...], (((1,), (1,)), ((), ())), preferred_element_type=jnp.float32)
        s = s * factor + jnp.concatenate([bias] * HEADS, axis=1)
        new = jnp.maximum(old, jnp.max(s, axis=0, keepdims=True))
        p = jnp.exp2(s - new)
        alpha = jnp.exp2(old - new)
        total = total * alpha + jnp.sum(p, axis=0, keepdims=True)
        acc[...] = acc[...] * alpha + lax.dot_general(
            value, p.astype(jnp.bfloat16), (((0,), (0,)), ((), ())), preferred_element_type=jnp.float32
        )
        return new, total

    wide = (1, HEADS * ROWS)
    _, total = lax.fori_loop(
        0, (ctx - block0 + STEP) // STEP, step, (jnp.full(wide, NEG, jnp.float32), jnp.zeros(wide, jnp.float32))
    )
    mixed = acc[...] / total
    for h in range(HEADS):
        context[:, h * HD : (h + 1) * HD] = jnp.transpose(mixed[:, h * ROWS : (h + 1) * ROWS]).astype(jnp.bfloat16)

    projected = jnp.sum(summed[...].astype(jnp.float32), axis=0)
    replica = lax.broadcasted_iota(jnp.int32, next_hidden.shape, 0)
    rows = jnp.zeros(next_hidden.shape, jnp.float32)
    for d in range(NDOC):
        rows = jnp.where(replica == replica_of[d], projected[d : d + 1], rows)
    next_hidden[...] = rows.astype(jnp.bfloat16)

    asked = jnp.int32(0)
    start = jnp.int32(0)
    length = jnp.int32(0)
    for d in range(NDOC):
        mine = replica_of[d] == ctx
        asked = jnp.where(mine, 1, asked)
        start = jnp.where(mine, starts[d], start)
        length = jnp.where(mine, ends[d] - starts[d], length)

    @pl.when(asked == 0)
    def _():
        replica_keys[...] = jnp.zeros_like(replica_keys)
        replica_values[...] = jnp.zeros_like(replica_values)

    @pl.when(asked == 1)
    def _():
        offset = lax.rem(start, ROWS)
        begin = start // ROWS
        r = lax.broadcasted_iota(jnp.int32, (2 * ROWS, ROWS), 0)
        s = lax.broadcasted_iota(jnp.int32, (2 * ROWS, ROWS), 1)
        hot = (r == s + offset).astype(jnp.bfloat16)
        slot = lax.broadcasted_iota(jnp.int32, (HD // 2, ROWS), 1)
        for i in range(MOST // ROWS):
            at = jnp.minimum(begin + i, NB - 1)
            live = slot + i * ROWS < length
            for which, out in ((0, replica_keys), (1, replica_values)):
                source = cache[which, pl.ds(at, 2)].reshape(2 * ROWS, HD)
                moved = lax.dot_general(source, hot, (((0,), (0,)), ((), ())), preferred_element_type=jnp.float32)
                moved = jnp.where(core == 0, moved[: HD // 2], moved[HD // 2 :])
                out[:, i * ROWS : (i + 1) * ROWS] = jnp.where(live, moved, 0.0).astype(jnp.bfloat16)


def prefill(replica_of, doc_ids, queries, summed, parts):
    vmem = pl.BlockSpec(memory_space=pltpu.VMEM)
    return pl.pallas_call(
        prefill_kernel,
        out_shape=(
            jax.ShapeDtypeStruct((ROWS, HEADS * HD), jnp.bfloat16),
            jax.ShapeDtypeStruct((NB, summed.shape[2]), jnp.bfloat16),
            jax.ShapeDtypeStruct((HD // 2, MOST), jnp.bfloat16),
            jax.ShapeDtypeStruct((HD // 2, MOST), jnp.bfloat16),
        ),
        in_specs=[pl.BlockSpec(memory_space=pltpu.SMEM)] + [vmem] * 8,
        scratch_shapes=[
            pltpu.VMEM((2, NB + STEP - 1, ROWS, HD), jnp.bfloat16),
            pltpu.VMEM((HEADS * ROWS, HD), jnp.bfloat16),
            pltpu.VMEM((HD, HEADS * ROWS), jnp.float32),
        ],
        compiler_params=pltpu.CompilerParams(vmem_limit_bytes=16 * 1024 * 1024),
        cost_estimate=pl.CostEstimate(flops=10**6, bytes_accessed=10**5, transcendentals=10**3),
        name="prefill",
    )(replica_of, doc_ids, queries, summed, *parts)


def from_sides(a, by):
    pairs = []
    for yh in range(2):
        for z in range(16):
            for t in range(16):
                core = t % 2
                source = (z + (by if core == 0 else -by)) % 16
                pairs.append(((yh * 16 + source) * 16 + t, (yh * 16 + z) * 16 + t))
    return lax.ppermute(a, CTX + TP, pairs)


def local(queries, keys, values, doc_ids, replica_of, step_query, step_key, step_value, out_weight):
    half = lax.all_gather(pick(keys, values), "z1", axis=0)
    far = lax.all_gather(half, ("yh", "c"), axis=0).reshape(2, 2, 4, ROWS, HD)
    near = from_sides(far, 1)
    blocks = doc_ids.reshape(NB, ROWS)
    decoded = lax.all_to_all(class_part(blocks, step_query, far), "z0", 0, 0)
    across = from_sides(lax.dynamic_slice_in_dim(far, lax.axis_index("c"), 1, 0), 2)
    terms = project(decoded, step_query, step_key, step_value, out_weight)
    others = [lax.all_gather(near[yh], "c", axis=0) for yh in range(2)]
    summed = lax.all_to_all(terms, TP, 0, 0)
    across, *others = lax.optimization_barrier((across, *others))
    across, summed = lax.optimization_barrier((lax.all_gather(across[0], "c", axis=0), summed))
    parts = [far, near, across, *others]
    context, next_hidden, replica_keys, replica_values = prefill(replica_of, blocks, queries, summed, parts)
    return (context, next_hidden, replica_keys[None], replica_values[None])


def solution(mesh):
    fine = Mesh(np.asarray(mesh.devices).reshape(2, 4, 4, 4, 2, 2), CTX + TP)
    placed = (
        P(CTX, TP),
        P(CTX, None),
        P(CTX, None),
        P(),
        P(),
        P(None, TP),
        P(),
        P(),
        P(TP, CTX),
    )
    return jax.shard_map(
        local,
        mesh=fine,
        in_specs=placed,
        out_specs=(P(CTX, TP), P(None, CTX), P(CTX, TP, None), P(CTX, TP, None)),
        check_vma=False,
    )
```

```python
import math

import jax
import jax.numpy as jnp
import numpy as np
from jax import lax
from jax.experimental import pallas as pl
from jax.experimental.pallas import tpu as pltpu
from jax.sharding import Mesh
from jax.sharding import PartitionSpec as P

H = 96
KVH = 8
HD = 128
NDOC = 4
ROWS = 128
NB = 32
MOST = 2560
HEADS = 6
SCALE = 1.0 / math.sqrt(HD)
CTX = ("yh", "z1", "z0")
TP = ("x", "yl", "c")
NEG = -1e30


def position():
    z0 = lax.axis_index("z0")
    ctx = lax.axis_index("yh") * 16 + lax.axis_index("z1") * 4 + z0
    return ctx, lax.axis_index("c"), lax.axis_index("x") * 2 + lax.axis_index("yl"), z0


def pick_kernel(keys, values, out, sem):
    _, core, head, _ = position()
    columns = pl.ds(pl.multiple_of(head * HD, HD), HD)
    for which, source in ((0, keys), (1, values)):

        @pl.when(core == which)
        def _():
            copy = pltpu.make_async_copy(source.at[:, columns], out, sem)
            copy.start()
            copy.wait()


def pick(keys, values):
    return pl.pallas_call(
        pick_kernel,
        out_shape=pltpu.VMEM((ROWS, HD), jnp.bfloat16),
        in_specs=[pl.BlockSpec(memory_space=pltpu.HBM)] * 2,
        out_specs=pl.BlockSpec(memory_space=pltpu.VMEM),
        scratch_shapes=[pltpu.SemaphoreType.DMA],
        compiler_params=pltpu.CompilerParams(vmem_limit_bytes=60 * 1024 * 1024),
        name="pick",
    )(keys, values)


def doc_bounds(doc_ids):
    ids = doc_ids[...]
    starts = [jnp.int32(0)] + [jnp.sum((ids < d).astype(jnp.int32)) for d in range(1, NDOC)]
    return starts, starts[1:] + [jnp.int32(NB * ROWS)]


ROW = HEADS * NDOC
PAD = 32


def combine(parts):
    top = parts[0][1]
    for _, weight in parts[1:]:
        top = jnp.maximum(top, weight)
    shares = [jnp.exp(weight - top) for _, weight in parts]
    return sum(share * mixed for share, (mixed, _) in zip(shares, parts)) / sum(shares)


def class_part_kernel(doc_ids, step_query, far, out, query):
    z0 = position()[3]
    query[...] = jnp.zeros_like(query)
    steps = step_query[...].astype(jnp.float32)
    for h in range(HEADS):
        query[h * NDOC : (h + 1) * NDOC, :] = steps[:, h * HD : (h + 1) * HD]
    narrow = query[...].astype(jnp.bfloat16)
    starts, ends = doc_bounds(doc_ids)
    document = lax.broadcasted_iota(jnp.int32, (PAD, 1), 0) % NDOC
    low = jnp.zeros((PAD, 1), jnp.int32)
    high = jnp.zeros((PAD, 1), jnp.int32)
    for d in range(NDOC):
        low = jnp.where(document == d, starts[d], low)
        high = jnp.where(document == d, ends[d], high)
    at = lax.broadcasted_iota(jnp.int32, (1, 4 * ROWS), 1)
    at = at // ROWS * (4 * ROWS) + at % ROWS + z0 * ROWS
    scores, seen = [], []
    top = jnp.full((PAD, 1), NEG, jnp.float32)
    for yh in range(2):
        place = at + yh * (16 * ROWS)
        mask = (place >= low) & (place < high)
        keys = far[yh, 0].reshape(4 * ROWS, HD)
        s = lax.dot_general(narrow, keys, (((1,), (1,)), ((), ())), preferred_element_type=jnp.float32)
        s = jnp.where(mask, s * SCALE, NEG)
        top = jnp.maximum(top, jnp.max(s, axis=1, keepdims=True))
        scores.append(s)
        seen.append(mask)
    total = jnp.zeros((PAD, 1), jnp.float32)
    mixed = jnp.zeros((PAD, HD), jnp.float32)
    for yh in range(2):
        p = jnp.where(seen[yh], jnp.exp(scores[yh] - top), 0.0)
        total = total + jnp.sum(p, axis=1, keepdims=True)
        values = far[yh, 1].reshape(4 * ROWS, HD)
        mixed = mixed + jnp.dot(p.astype(jnp.bfloat16), values, preferred_element_type=jnp.float32)
    some = total > 0.0
    safe = jnp.where(some, total, 1.0)
    weight = jnp.where(some, top + jnp.log(safe), NEG)
    sub = lax.broadcasted_iota(jnp.int32, (PAD, HD), 0)
    lane = lax.broadcasted_iota(jnp.int32, (PAD, HD), 1)
    line = jnp.sum(jnp.where(sub == lane, weight, 0.0), axis=0, keepdims=True)
    part = jnp.where(sub == ROW, line, mixed / safe)
    for k in range(out.shape[0]):
        out[k] = part


def class_part(doc_ids, step_query, far):
    return pl.pallas_call(
        class_part_kernel,
        out_shape=pltpu.VMEM((4, PAD, HD), jnp.float32),
        scratch_shapes=[pltpu.VMEM((PAD, HD), jnp.float32)],
        compiler_params=pltpu.CompilerParams(vmem_limit_bytes=8 * 1024 * 1024),
        cost_estimate=pl.CostEstimate(flops=3 * 10**7, bytes_accessed=10**6, transcendentals=4 * 10**4),
        name="class_part",
    )(doc_ids, step_query, far)


def project_kernel(parts, step_query, step_key, step_value, weight, terms, product, mixed):
    head = position()[2]
    columns = pl.ds(pl.multiple_of(head * HD, HD), HD)
    steps = step_query[...].astype(jnp.float32)
    step_keys = step_key[:, columns].astype(jnp.float32)
    step_values = step_value[:, columns].astype(jnp.float32)
    for ref in (product, mixed):
        ref[ROW:PAD, :] = jnp.zeros((PAD - ROW, HD), jnp.float32)
    for h in range(HEADS):
        rows = slice(h * NDOC, (h + 1) * NDOC)
        product[rows, :] = steps[:, h * HD : (h + 1) * HD] * step_keys
        mixed[rows, :] = step_values
    sub = lax.broadcasted_iota(jnp.int32, (PAD, HD), 0)
    lane = lax.broadcasted_iota(jnp.int32, (PAD, HD), 1)
    found = [(mixed[...], jnp.sum(product[...], axis=1, keepdims=True) * SCALE)]
    for k in range(parts.shape[0]):
        part = parts[k]
        line = jnp.sum(jnp.where(sub == ROW, part, 0.0), axis=0, keepdims=True)
        found.append((part, jnp.sum(jnp.where(sub == lane, line, 0.0), axis=1, keepdims=True)))
    mixed[...] = combine(found)
    wide = jnp.concatenate([mixed[h * NDOC : (h + 1) * NDOC, :] for h in range(HEADS)], axis=1)
    wide = jnp.concatenate([wide, jnp.zeros_like(wide)], axis=0)
    term = jnp.dot(wide.astype(jnp.bfloat16), weight[...], preferred_element_type=jnp.float32).astype(terms.dtype)
    for k in range(16):
        terms[k] = term


def project(parts, step_query, step_key, step_value, weight):
    return pl.pallas_call(
        project_kernel,
        out_shape=pltpu.VMEM((16, 8, weight.shape[1]), jnp.bfloat16),
        scratch_shapes=[pltpu.VMEM((PAD, HD), jnp.float32)] * 2,
        compiler_params=pltpu.CompilerParams(vmem_limit_bytes=8 * 1024 * 1024),
        cost_estimate=pl.CostEstimate(flops=10**7, bytes_accessed=10**6, transcendentals=10**3),
        name="project",
    )(parts, step_query, step_key, step_value, weight)


STEP = 6


def prefill_kernel(
    replica_of, doc_ids, queries, summed, far, near, across, other0, other1,
    context, next_hidden, replica_keys, replica_values,
    cache, flat, acc,
):
    ctx, core, _, z0 = position()
    side = 1 - 2 * core
    for which in range(2):
        for g in range(4):
            for yh in range(2):
                at = yh * 16 + g * 4
                cache[which, at + z0] = far[yh, which, g]
                cache[which, at + lax.rem(z0 + 4 + side, 4)] = near[yh, which, g]
                cache[which, at + lax.rem(z0 + 4 - side, 4)] = (other0, other1)[yh][1 - core, which, g]
                cache[which, at + lax.rem(z0 + 2, 4)] = across[yh, which, g]
        for b in range(NB, NB + STEP - 1):
            cache[which, b] = jnp.zeros((ROWS, HD), jnp.bfloat16)
    starts, ends = doc_bounds(doc_ids)
    for h in range(HEADS):
        flat[h * ROWS : (h + 1) * ROWS, :] = queries[:, h * HD : (h + 1) * HD]

    row = ctx * ROWS + lax.broadcasted_iota(jnp.int32, (1, ROWS), 1)
    row_start = jnp.zeros((1, ROWS), jnp.int32)
    first = jnp.int32(0)
    for d in range(1, NDOC):
        row_start = jnp.where(row >= starts[d], starts[d], row_start)
        first = jnp.where(ctx * ROWS >= starts[d], starts[d], first)
    block0 = first // ROWS
    factor = SCALE * math.log2(math.e)
    acc[...] = jnp.zeros_like(acc)

    def step(i, carry):
        old, total = carry
        at = block0 + STEP * i
        key = cache[0, pl.ds(at, STEP)].reshape(STEP * ROWS, HD)
        value = cache[1, pl.ds(at, STEP)].reshape(STEP * ROWS, HD)
        place = at * ROWS + lax.broadcasted_iota(jnp.int32, (STEP * ROWS, ROWS), 0)
        bias = jnp.where((place <= row) & (place >= row_start), 0.0, NEG)
        s = lax.dot_general(key, flat[...], (((1,), (1,)), ((), ())), preferred_element_type=jnp.float32)
        s = s * factor + jnp.concatenate([bias] * HEADS, axis=1)
        new = jnp.maximum(old, jnp.max(s, axis=0, keepdims=True))
        p = jnp.exp2(s - new)
        alpha = jnp.exp2(old - new)
        total = total * alpha + jnp.sum(p, axis=0, keepdims=True)
        acc[...] = acc[...] * alpha + lax.dot_general(
            value, p.astype(jnp.bfloat16), (((0,), (0,)), ((), ())), preferred_element_type=jnp.float32
        )
        return new, total

    wide = (1, HEADS * ROWS)
    _, total = lax.fori_loop(
        0, (ctx - block0 + STEP) // STEP, step, (jnp.full(wide, NEG, jnp.float32), jnp.zeros(wide, jnp.float32))
    )
    mixed = acc[...] / total
    for h in range(HEADS):
        context[:, h * HD : (h + 1) * HD] = jnp.transpose(mixed[:, h * ROWS : (h + 1) * ROWS]).astype(jnp.bfloat16)

    projected = jnp.sum(summed[...].astype(jnp.float32), axis=0)
    replica = lax.broadcasted_iota(jnp.int32, next_hidden.shape, 0)
    rows = jnp.zeros(next_hidden.shape, jnp.float32)
    for d in range(NDOC):
        rows = jnp.where(replica == replica_of[d], projected[d : d + 1], rows)
    next_hidden[...] = rows.astype(jnp.bfloat16)

    asked = jnp.int32(0)
    start = jnp.int32(0)
    length = jnp.int32(0)
    for d in range(NDOC):
        mine = replica_of[d] == ctx
        asked = jnp.where(mine, 1, asked)
        start = jnp.where(mine, starts[d], start)
        length = jnp.where(mine, ends[d] - starts[d], length)

    @pl.when(asked == 0)
    def _():
        replica_keys[...] = jnp.zeros_like(replica_keys)
        replica_values[...] = jnp.zeros_like(replica_values)

    @pl.when(asked == 1)
    def _():
        offset = lax.rem(start, ROWS)
        begin = start // ROWS
        r = lax.broadcasted_iota(jnp.int32, (2 * ROWS, ROWS), 0)
        s = lax.broadcasted_iota(jnp.int32, (2 * ROWS, ROWS), 1)
        hot = (r == s + offset).astype(jnp.bfloat16)
        slot = lax.broadcasted_iota(jnp.int32, (HD // 2, ROWS), 1)
        for i in range(MOST // ROWS):
            at = jnp.minimum(begin + i, NB - 1)
            live = slot + i * ROWS < length
            for which, out in ((0, replica_keys), (1, replica_values)):
                source = cache[which, pl.ds(at, 2)].reshape(2 * ROWS, HD)
                moved = lax.dot_general(source, hot, (((0,), (0,)), ((), ())), preferred_element_type=jnp.float32)
                moved = jnp.where(core == 0, moved[: HD // 2], moved[HD // 2 :])
                out[:, i * ROWS : (i + 1) * ROWS] = jnp.where(live, moved, 0.0).astype(jnp.bfloat16)


def prefill(replica_of, doc_ids, queries, summed, parts):
    vmem = pl.BlockSpec(memory_space=pltpu.VMEM)
    return pl.pallas_call(
        prefill_kernel,
        out_shape=(
            jax.ShapeDtypeStruct((ROWS, HEADS * HD), jnp.bfloat16),
            jax.ShapeDtypeStruct((NB, summed.shape[2]), jnp.bfloat16),
            jax.ShapeDtypeStruct((HD // 2, MOST), jnp.bfloat16),
            jax.ShapeDtypeStruct((HD // 2, MOST), jnp.bfloat16),
        ),
        in_specs=[pl.BlockSpec(memory_space=pltpu.SMEM)] + [vmem] * 8,
        scratch_shapes=[
            pltpu.VMEM((2, NB + STEP - 1, ROWS, HD), jnp.bfloat16),
            pltpu.VMEM((HEADS * ROWS, HD), jnp.bfloat16),
            pltpu.VMEM((HD, HEADS * ROWS), jnp.float32),
        ],
        compiler_params=pltpu.CompilerParams(vmem_limit_bytes=16 * 1024 * 1024),
        cost_estimate=pl.CostEstimate(flops=10**6, bytes_accessed=10**5, transcendentals=10**3),
        name="prefill",
    )(replica_of, doc_ids, queries, summed, *parts)


def from_sides(a, by):
    pairs = []
    for yh in range(2):
        for z in range(16):
            for t in range(16):
                core = t % 2
                source = (z + (by if core == 0 else -by)) % 16
                pairs.append(((yh * 16 + source) * 16 + t, (yh * 16 + z) * 16 + t))
    return lax.ppermute(a, CTX + TP, pairs)


def local(queries, keys, values, doc_ids, replica_of, step_query, step_key, step_value, out_weight):
    half = lax.all_gather(pick(keys, values), "z1", axis=0)
    far = lax.all_gather(half, ("yh", "c"), axis=0).reshape(2, 2, 4, ROWS, HD)
    near = from_sides(far, 1)
    blocks = doc_ids.reshape(NB, ROWS)
    decoded = lax.all_to_all(class_part(blocks, step_query, far), "z0", 0, 0)
    across = from_sides(lax.dynamic_slice_in_dim(far, lax.axis_index("c"), 1, 0), 2)
    terms = project(decoded, step_query, step_key, step_value, out_weight)
    others = [lax.all_gather(near[yh], "c", axis=0) for yh in range(2)]
    summed = lax.all_to_all(terms, TP, 0, 0)
    across, *others = lax.optimization_barrier((across, *others))
    across, summed = lax.optimization_barrier((lax.all_gather(across[0], "c", axis=0), summed))
    parts = [far, near, across, *others]
    context, next_hidden, replica_keys, replica_values = prefill(replica_of, blocks, queries, summed, parts)
    return (context, next_hidden, replica_keys[None], replica_values[None])


def solution(mesh):
    fine = Mesh(np.asarray(mesh.devices).reshape(2, 4, 4, 4, 2, 2), CTX + TP)
    placed = (
        P(CTX, TP),
        P(CTX, None),
        P(CTX, None),
        P(),
        P(),
        P(None, TP),
        P(),
        P(),
        P(TP, CTX),
    )
    return jax.shard_map(
        local,
        mesh=fine,
        in_specs=placed,
        out_specs=(P(CTX, TP), P(None, CTX), P(CTX, TP, None), P(CTX, TP, None)),
        check_vma=False,
    )
```
